128 devices in a mesh: dp: 128 (over z, y, x, core).
Axes of the slice: x: 4, y: 4, z: 4, core: 2. Of those that a mesh axis runs over, the one named last changes fastest.
Arguments:
- latents: bfloat16 [256, 256, 384], P('dp'), may hold values from -4 to 4
- condition: bfloat16 [256, 384], P('dp'), may hold values from -3 to 3
- cotangent: bfloat16 [256, 256, 384], P('dp'), may hold values from -4 to 4
- slot_table: int32 [128, 2], P('dp'), may hold values from 0 to 1, each once within a row
- counts: int32 [128], P('dp'), may hold values from 1 to 2, as said below
- w_ada: bfloat16 [2, 384, 2304], P(None, 'dp'), may hold values from -0.09 to 0.09
- b_ada: bfloat16 [2, 2304], P(None, 'dp'), may hold values from -0.5 to 0.5
- w_qkv: bfloat16 [2, 384, 1152], P(None, 'dp'), may hold values from -0.3125 to 0.3125
- b_qv: bfloat16 [2, 768], P(None, 'dp'), may hold values from -0.5 to 0.5
- w_proj: bfloat16 [2, 384, 384], P(None, 'dp'), may hold values from -1.25 to 1.25
- b_proj: bfloat16 [2, 384], P(None, 'dp'), may hold values from -0.5 to 0.5
- w_fc1: bfloat16 [2, 384, 1536], P(None, 'dp'), may hold values from -0.3125 to 0.3125
- b_fc1: bfloat16 [2, 1536], P(None, 'dp'), may hold values from -0.5 to 0.5
- w_fc2: bfloat16 [2, 1536, 384], P(None, 'dp'), may hold values from -0.15625 to 0.15625
- b_fc2: bfloat16 [2, 384], P(None, 'dp'), may hold values from -0.5 to 0.5
Outputs:
- activations: bfloat16 [256, 256, 384], P('dp')
- grad_latents: bfloat16 [256, 256, 384], P('dp')
- grad_condition: float32 [256, 384], P('dp')
- grad_w_ada: float32 [2, 384, 2304], P(None, 'dp')
- grad_b_ada: float32 [2, 2304], P(None, 'dp')
- grad_w_qkv: float32 [2, 384, 1152], P(None, 'dp')
- grad_b_qv: float32 [2, 768], P(None, 'dp')
- grad_w_proj: float32 [2, 384, 384], P(None, 'dp')
- grad_b_proj: float32 [2, 384], P(None, 'dp')
- grad_w_fc1: float32 [2, 384, 1536], P(None, 'dp')
- grad_b_fc1: float32 [2, 1536], P(None, 'dp')
- grad_w_fc2: float32 [2, 1536, 384], P(None, 'dp')
- grad_b_fc2: float32 [2, 384], P(None, 'dp')
The draws below stay inside these ranges and needn't reach their ends.
Inputs may be any that keep to these rules, and one draw needn't show every extreme that they name: Each row of slot_table lists the device's 2 latent slots, each once. `counts`: some device runs 2 micro-batches and some device runs one.
All inputs are finite; a program needn't handle non-finite values.
Results may differ from the reference program's by a relative error of at most 0.014.
Values may be sent and summed in bfloat16 or wider, within the bound.
A program may use at most 192 MiB of HBM per device.

```python
import jax
import jax.numpy as jnp
from jax import lax

D = 384
HEADS = 6
FF = 1536
L = 256
LAYERS = 2
LAT_DEV = 2
RANKS = 128
LATENTS = 256


def draw_counts(key, part):
    key = jax.random.fold_in(key, 7)
    key_base, key_high, key_low = jax.random.split(key, 3)
    values = jax.random.randint(key_base, (RANKS,), 1, LAT_DEV + 1)
    high_at = jax.random.randint(key_high, (), 0, RANKS)
    low_at = (high_at + 1 + jax.random.randint(key_low, (), 0, RANKS - 1)) % RANKS
    values = values.at[high_at].set(LAT_DEV)
    values = values.at[low_at].set(1)
    return values.astype(jnp.int32)


def draw_condition(key, part):
    key = jax.random.fold_in(key, 11)
    values = jax.random.normal(key, (LATENTS, D), jnp.float32)
    return jnp.clip(values, -3.0, 3.0).astype(jnp.bfloat16)


def draw_w_ada(key, part):
    key = jax.random.fold_in(key, 13)
    values = jax.random.uniform(key, (LAYERS, D, 6 * D), jnp.float32, -1.7320508, 1.7320508)
    return (values * D ** (-0.5)).astype(jnp.bfloat16)


def block_scale(key, shape, cuts, low, largest):
    def one(axis_at, parts):
        steps = jax.random.uniform(jax.random.fold_in(jax.random.fold_in(key, 6), axis_at), (parts,), jnp.float32, low / len(cuts), largest / len(cuts))
        return jnp.repeat(jnp.exp(steps), shape[axis_at] // parts).reshape((-1,) + (1,) * (len(shape) - axis_at - 1))

    factor_of = one(*cuts[0])
    for cut in cuts[1:]:
        factor_of = factor_of * one(*cut)
    return factor_of


def noise(rng, shape, scale, limit, cuts=(), kind=jnp.bfloat16):
    entries = jax.random.normal(rng, shape, jnp.float32) * scale
    if len(cuts) > 0:
        entries = block_scale(rng, shape, cuts, -0.22, 0.18) * entries
    return jnp.clip(entries, min=-limit, max=limit).astype(kind)


def setup_inputs(seed: int = 0) -> dict:
    splits = jax.random.split(jax.random.key(seed), 16)
    return {
        "latents": noise(splits[0], (LATENTS, L, D), 1.0, 4.0, ((0, 128),)),
        "condition": draw_condition(jax.random.fold_in(splits[15], 71), 0),
        "cotangent": noise(splits[2], (LATENTS, L, D), 1.0, 4.0, ((0, 128),)),
        "slot_table": jax.vmap(lambda own: jax.random.permutation(own, LAT_DEV))(jax.random.split(splits[3], RANKS)).reshape((RANKS, LAT_DEV)).astype(jnp.int32),
        "counts": draw_counts(jax.random.fold_in(splits[15], 71), 0),
        "w_ada": draw_w_ada(jax.random.fold_in(splits[15], 71), 0),
        "b_ada": jnp.clip(jax.random.uniform(splits[6], (LAYERS, 6 * D), jnp.float32, -0.5, 0.5) * block_scale(splits[6], (LAYERS, 6 * D), ((1, 128),), -0.4, 0.0), -0.5, 0.5).astype(jnp.bfloat16),
        "w_qkv": noise(splits[7], (LAYERS, D, 3 * D), D ** -0.5, 0.3125, ((1, 128),)),
        "b_qv": jnp.clip(jax.random.uniform(splits[8], (LAYERS, 2 * D), jnp.float32, -0.5, 0.5) * block_scale(splits[8], (LAYERS, 2 * D), ((1, 128),), -0.4, 0.0), -0.5, 0.5).astype(jnp.bfloat16),
        "w_proj": noise(splits[9], (LAYERS, D, D), (D // 16) ** -0.5, 1.25, ((1, 128),)),
        "b_proj": jnp.clip(jax.random.uniform(splits[10], (LAYERS, D), jnp.float32, -0.5, 0.5) * block_scale(splits[10], (LAYERS, D), ((1, 128),), -0.4, 0.0), -0.5, 0.5).astype(jnp.bfloat16),
        "w_fc1": noise(splits[11], (LAYERS, D, FF), D ** -0.5, 0.3125, ((1, 128),)),
        "b_fc1": jnp.clip(jax.random.uniform(splits[12], (LAYERS, FF), jnp.float32, -0.5, 0.5) * block_scale(splits[12], (LAYERS, FF), ((1, 128),), -0.4, 0.0), -0.5, 0.5).astype(jnp.bfloat16),
        "w_fc2": noise(splits[13], (LAYERS, FF, D), FF ** -0.5, 0.15625, ((1, 128),)),
        "b_fc2": jnp.clip(jax.random.uniform(splits[14], (LAYERS, D), jnp.float32, -0.5, 0.5) * block_scale(splits[14], (LAYERS, D), ((1, 128),), -0.4, 0.0), -0.5, 0.5).astype(jnp.bfloat16),
    }


highest = lax.Precision.HIGHEST
eps_norm = 1e-06
gelu_coef = 0.7978845608028654

@jax.custom_vjp
def low(v):
    return lax.optimization_barrier(v.astype(jnp.bfloat16)).astype(jnp.float32)

@jax.custom_vjp
def low_back(v):
    return v

def low_keep(v):
    return (low(v), None)

def low_pass(kept, grad):
    return (grad,)

def back_keep(v):
    return (v, None)

def back_low(kept, grad):
    return (low(grad),)
low.defvjp(low_keep, low_pass)
low_back.defvjp(back_keep, back_low)

def layer_norm(stream):
    average = lax.optimization_barrier(jnp.mean(stream, axis=-1, keepdims=True))
    centred = stream - average
    variance = lax.optimization_barrier(jnp.mean(centred * centred, axis=-1, keepdims=True))
    return centred * lax.rsqrt(variance + eps_norm)

def modulate(stream, shift, scale):
    return layer_norm(stream) * (1.0 + scale) + shift

def gelu_tanh(hidden):
    return 0.5 * hidden * (1.0 + jnp.tanh(gelu_coef * (hidden + 0.044715 * hidden * hidden * hidden)))

def one_layer(stream, cond, weights):
    w_ada, b_ada, w_qkv, b_qv, w_proj, b_proj, w_fc1, b_fc1, w_fc2, b_fc2 = weights
    groups, length, width = stream.shape
    head_size = width // HEADS
    silu_cond = low(jax.nn.silu(cond))
    modulation = jnp.dot(silu_cond, w_ada, precision=highest) + b_ada
    pieces = [piece[:, None, :] for piece in jnp.split(modulation, 6, axis=-1)]
    shift_attn, scale_attn, gate_attn, shift_mlp, scale_mlp, gate_mlp = pieces
    normed = low(modulate(stream, shift_attn, scale_attn))
    bias_qkv = jnp.concatenate([b_qv[:width], jnp.zeros((width,), jnp.float32), b_qv[width:]])
    projected = low_back(low(jnp.einsum('gld,de->gle', normed, w_qkv, precision=highest) + bias_qkv))
    queries = projected[..., :width].reshape(groups, length, HEADS, head_size)
    key_rows = projected[..., width:2 * width].reshape(groups, length, HEADS, head_size)
    values = projected[..., 2 * width:].reshape(groups, length, HEADS, head_size)
    scores = low_back(jnp.einsum('gqhe,gkhe->ghqk', queries, key_rows, precision=highest) * head_size ** (-0.5))
    row_peak = lax.optimization_barrier(jnp.max(scores, axis=-1, keepdims=True))
    exponent = jnp.exp(scores - row_peak)
    attention = low(exponent / lax.optimization_barrier(jnp.sum(exponent, axis=-1, keepdims=True)))
    attended = jnp.einsum('ghqk,gkhe->gqhe', attention, values, precision=highest).reshape(groups, length, width)
    attended = low_back(low(attended))
    branch = low_back(jnp.einsum('gld,de->gle', attended, w_proj, precision=highest) + b_proj)
    middle = stream + gate_attn * branch
    normed_mlp = low(modulate(middle, shift_mlp, scale_mlp))
    hidden = low_back(jnp.einsum('gld,df->glf', normed_mlp, w_fc1, precision=highest) + b_fc1)
    activated = low(gelu_tanh(hidden))
    output = low_back(jnp.einsum('glf,fd->gld', activated, w_fc2, precision=highest) + b_fc2)
    return middle + gate_mlp * output

def stack_layers(stream, cond, params):
    for index in range(LAYERS):
        stream = one_layer(stream, cond, tuple((array[index] for array in params)))
    return stream

def reference(latents, condition, cotangent, slot_table, counts, w_ada, b_ada, w_qkv, b_qv, w_proj, b_proj, w_fc1, b_fc1, w_fc2, b_fc2):
    params = tuple((array.astype(jnp.float32) for array in (w_ada, b_ada, w_qkv, b_qv, w_proj, b_proj, w_fc1, b_fc1, w_fc2, b_fc2)))
    position = jnp.arange(LAT_DEV, dtype=jnp.int32)
    chosen = (slot_table[:, :, None] == position[None, None, :]) & (position[None, :, None] < counts[:, None, None])
    live_flags = jnp.any(chosen, axis=1).reshape(LATENTS).astype(jnp.float32)
    stream_all = latents.astype(jnp.float32)
    cond_all = condition.astype(jnp.float32)
    cot_all = cotangent.astype(jnp.float32)
    group_size = 16

    def group_step(totals, group_index):
        start = (group_index * group_size).astype(jnp.int32)
        block_stream = lax.dynamic_slice_in_dim(stream_all, start, group_size, 0)
        block_cond = lax.dynamic_slice_in_dim(cond_all, start, group_size, 0)
        block_cot = lax.dynamic_slice_in_dim(cot_all, start, group_size, 0)
        block_live = lax.dynamic_slice_in_dim(live_flags, start, group_size, 0)[:, None, None]
        result, pullback = jax.vjp(stack_layers, block_stream, block_cond, params)
        grad_stream, grad_cond, grad_params = pullback(block_cot * block_live)
        totals = jax.tree.map(jnp.add, totals, grad_params)
        return (totals, (result * block_live, grad_stream, grad_cond))
    zero_totals = tuple((jnp.zeros_like(array) for array in params))
    totals, gathered = lax.scan(group_step, zero_totals, jnp.arange(LATENTS // group_size, dtype=jnp.int32))
    results, grad_streams, grad_conds = gathered
    results = results.reshape(LATENTS, L, D).astype(jnp.bfloat16)
    grad_streams = grad_streams.reshape(LATENTS, L, D).astype(jnp.bfloat16)
    grad_conds = grad_conds.reshape(LATENTS, D)
    g_w_ada, g_b_ada, g_w_qkv, g_b_qv, g_w_proj, g_b_proj, g_w_fc1, g_b_fc1, g_w_fc2, g_b_fc2 = totals
    return (results, grad_streams, grad_conds, g_w_ada, g_b_ada, g_w_qkv, g_b_qv, g_w_proj, g_b_proj, g_w_fc1, g_b_fc1, g_w_fc2, g_b_fc2)
```

```python
import functools
import jax
import jax.numpy as jnp
from jax import lax
from jax.experimental import pallas as pl
from jax.experimental.pallas import tpu as pltpu
from jax.sharding import PartitionSpec as P
import numpy as np

f32 = jnp.float32
bf16 = jnp.bfloat16
D = 384
HEADS = 6
FF = 1536
LAYERS = 2
LEN = 256
SLOTS = 2
ROWS = SLOTS * LEN
CHUNK = 64
STEPS = ROWS // CHUNK
EPS = 1e-06
GELU = 0.7978845608028654
VMEM_BYTES = 65280 * 1024


def mm(a, b):
    return lax.dot_general(a, b, (((1,), (0,)), ((), ())), preferred_element_type=f32)


def mm_t(a, b):
    return lax.dot_general(a, b, (((1,), (1,)), ((), ())), preferred_element_type=f32)


def t_mm(a, b):
    return lax.dot_general(a, b, (((0,), (0,)), ((), ())), preferred_element_type=f32)


def row_chunks(step):
    @pl.loop(0, STEPS)
    def _(i):
        rows = pl.ds(pl.multiple_of(i * CHUNK, CHUNK), CHUNK)
        slot = i // (STEPS // SLOTS)
        step(rows, slot)


def norm_parts(x):
    mean = jnp.mean(x, axis=-1, keepdims=True)
    centred = x - mean
    var = jnp.mean(centred * centred, axis=-1, keepdims=True)
    inv = lax.rsqrt(var + EPS)
    return centred * inv, inv


def norm_pull(u, n, inv):
    mean_u = jnp.mean(u, axis=-1, keepdims=True)
    mean_un = jnp.mean(u * n, axis=-1, keepdims=True)
    return inv * (u - mean_u - n * mean_un)


def keep_half(x, odd):
    lane = lax.broadcasted_iota(jnp.int32, (1, x.shape[1]), 1)
    mask = (lane >= 64) if odd else (lane < 64)
    return jnp.where(mask, x, jnp.zeros_like(x))


def keep_inv(S, rows, k, inv):
    lane = lax.broadcasted_iota(jnp.int32, (CHUNK, 128), 1)
    S["inv"][rows, :] = jnp.where(lane == k, inv, S["inv"][rows, :])


def mod_part(S, l, slot, k):
    return S["mod"][l, pl.ds(slot, 1), k * D : (k + 1) * D]


def forward_attention(l, W, S, tick):
    S["mod"][l] = mm(S["silu"][...], W["ada"][l]) + W["b_ada"][l]

    def prep(rows, slot):
        x = (S["lat"] if l == 0 else S["h"])[rows, :].astype(f32)
        n, inv = norm_parts(x)
        S["n_a"][l, rows, :] = n.astype(bf16)
        keep_inv(S, rows, l, inv)
        S["normed"][l, rows, :] = (
            n * (1.0 + mod_part(S, l, slot, 1)) + mod_part(S, l, slot, 0)
        ).astype(bf16)

    row_chunks(prep)
    tick()
    for k in range(3):
        cols = slice(k * D, (k + 1) * D)
        out = mm(S["normed"][l], W["qkv"][l, :, cols])
        if k != 1:
            b = W["b_qv"][l, :, 0:D] if k == 0 else W["b_qv"][l, :, D:]
            out = out + b
        S["proj"][l, :, cols] = out.astype(bf16)
    tick()
    for slot in range(SLOTS):
        rows = slice(slot * LEN, slot * LEN + LEN)
        for pair in range(3):
            lanes = slice(pair * 128, pair * 128 + 128)
            q = S["proj"][l, rows, lanes]
            k = S["proj"][l, rows, D + pair * 128 : D + pair * 128 + 128]
            v = S["proj"][l, rows, 2 * D + pair * 128 : 2 * D + pair * 128 + 128]
            att = None
            for odd in range(2):
                s = mm_t(keep_half(q, odd), k) * 0.125
                e = jnp.exp(s - jnp.max(s, axis=-1, keepdims=True))
                p = (e / jnp.sum(e, axis=-1, keepdims=True)).astype(bf16)
                S["prob"][l, slot * HEADS + pair * 2 + odd] = p
                term = mm(p, keep_half(v, odd))
                att = term if att is None else att + term
            S["att"][l, rows, lanes] = att.astype(bf16)
        tick()
    S["gn"][...] = mm(S["att"][l], W["proj"][l]) + W["b_proj"][l]
    tick()


def forward_mlp(l, W, S, tick):
    def middle(rows, slot):
        x = (S["lat"] if l == 0 else S["h"])[rows, :].astype(f32)
        branch = S["gn"][rows, :]
        S["branch"][l, rows, :] = branch.astype(bf16)
        m = x + mod_part(S, l, slot, 2) * branch
        S["h"][rows, :] = m
        n, inv = norm_parts(m)
        S["n_m"][l, rows, :] = n.astype(bf16)
        keep_inv(S, rows, LAYERS + l, inv)
        S["normed_m"][l, rows, :] = (
            n * (1.0 + mod_part(S, l, slot, 4)) + mod_part(S, l, slot, 3)
        ).astype(bf16)

    row_chunks(middle)
    tick()
    for part in range(2):

        @pl.loop(0, FF // 512)
        def _(j):
            cols = pl.ds(pl.multiple_of(part * (FF // 2) + j * 256, 256), 256)
            x = mm(S["normed_m"][l], W["fc1"][l, :, cols]) + W["b_fc1"][l, :, cols]
            x2 = x * x
            t = jnp.tanh(GELU * (x + 0.044715 * (x2 * x)))
            half = 0.5 * (1.0 + t)
            S["activated"][l, :, cols] = (x * half).astype(bf16)
            slope = half + 0.5 * x * (1.0 - t * t) * (GELU * (1.0 + 3 * 0.044715 * x2))
            S["slope"][l, :, cols] = slope.astype(bf16)

        tick()
    S["gn"][...] = mm(S["activated"][l], W["fc2"][l]) + W["b_fc2"][l]

    def finish(rows, slot):
        output = S["gn"][rows, :]
        S["output"][l, rows, :] = output.astype(bf16)
        r = S["h"][rows, :] + mod_part(S, l, slot, 5) * output
        if l == LAYERS - 1:
            S["act_out"][rows, :] = (r * S["live"][pl.ds(slot, 1), :]).astype(bf16)
        else:
            S["h"][rows, :] = r

    row_chunks(finish)
    tick()


def add_mod(S, l, slot, k, value):
    cols = slice(k * D, (k + 1) * D)
    S["gmod"][l, pl.ds(slot, 1), cols] += jnp.sum(value, axis=0, keepdims=True)


def backward_mlp(l, W, S, G, tick):
    ones = jnp.ones((8, ROWS), bf16)
    S["gmod"][l] = jnp.zeros((8, 6 * D), f32)

    def start(rows, slot):
        if l == LAYERS - 1:
            g = S["cot"][rows, :].astype(f32) * S["live"][pl.ds(slot, 1), :]
            S["h"][rows, :] = g
        else:
            g = S["h"][rows, :]
        add_mod(S, l, slot, 5, g * S["output"][l, rows, :].astype(f32))
        S["go"][rows, :] = (mod_part(S, l, slot, 5) * g).astype(bf16)

    row_chunks(start)
    go = S["go"]
    G["b_fc2"][...] = mm(ones, go[...])
    tick()
    for part in range(2):

        @pl.loop(0, FF // 512)
        def _(j):
            cols = pl.ds(pl.multiple_of(part * (FF // 2) + j * 256, 256), 256)
            gh = mm_t(go[...], W["fc2"][l, cols, :]) * S["slope"][l, :, cols].astype(f32)
            gh = gh.astype(bf16)
            G["fc2"][cols, :] = t_mm(S["activated"][l, :, cols], go[...]).astype(bf16)
            S["activated"][l, :, cols] = gh
            G["fc1"][:, cols] = t_mm(S["normed_m"][l], gh).astype(bf16)
            G["b_fc1"][:, cols] = mm(ones, gh)

        tick()


def backward_middle(l, W, S, G, tick):
    ones = jnp.ones((8, ROWS), bf16)
    go = S["go"]
    S["gn"][...] = mm_t(S["activated"][l], W["fc1"][l])

    def mid(rows, slot):
        gn = S["gn"][rows, :]
        n = S["n_m"][l, rows, :].astype(f32)
        inv = S["inv"][rows, LAYERS + l : LAYERS + l + 1]
        add_mod(S, l, slot, 3, gn)
        add_mod(S, l, slot, 4, gn * n)
        gm = S["h"][rows, :] + norm_pull((1.0 + mod_part(S, l, slot, 4)) * gn, n, inv)
        S["h"][rows, :] = gm
        add_mod(S, l, slot, 2, gm * S["branch"][l, rows, :].astype(f32))
        S["go"][rows, :] = (mod_part(S, l, slot, 2) * gm).astype(bf16)

    row_chunks(mid)
    tick()
    G["b_proj"][...] = mm(ones, go[...])
    G["proj"][...] = t_mm(S["att"][l], go[...]).astype(bf16)
    S["att"][l] = mm_t(go[...], W["proj"][l]).astype(bf16)
    tick()
    for slot in range(SLOTS):
        rows = slice(slot * LEN, slot * LEN + LEN)
        for pair in range(3):
            lanes = slice(pair * 128, pair * 128 + 128)
            kl = slice(D + pair * 128, D + pair * 128 + 128)
            vl = slice(2 * D + pair * 128, 2 * D + pair * 128 + 128)
            q = S["proj"][l, rows, lanes]
            k = S["proj"][l, rows, kl]
            v = S["proj"][l, rows, vl]
            ga = S["att"][l, rows, lanes]
            gq = gk = gv = None
            for odd in range(2):
                low = S["prob"][l, slot * HEADS + pair * 2 + odd]
                p = low.astype(f32)
                ga_h = keep_half(ga, odd)
                gp = mm_t(ga_h, v)
                dot = jnp.sum(p * gp, axis=-1, keepdims=True)
                gs = (p * (gp - dot)).astype(bf16)
                tv = t_mm(low, ga_h)
                tq = mm(gs, keep_half(k, odd))
                tk = t_mm(gs, keep_half(q, odd))
                gv = tv if gv is None else gv + tv
                gq = tq if gq is None else gq + tq
                gk = tk if gk is None else gk + tk
            S["proj"][l, rows, lanes] = (gq * 0.125).astype(bf16)
            S["proj"][l, rows, kl] = (gk * 0.125).astype(bf16)
            S["proj"][l, rows, vl] = gv.astype(bf16)
        tick()


def backward_end(l, W, S, G, tick):
    ones = jnp.ones((8, ROWS), bf16)
    for k in range(3):
        cols = slice(k * D, (k + 1) * D)
        gpk = S["proj"][l, :, cols]
        G["qkv"][:, cols] = t_mm(S["normed"][l], gpk).astype(bf16)
        if k != 1:
            G["b_qv"][:, (k // 2) * D : (k // 2 + 1) * D] = mm(ones, gpk)
    S["gn"][...] = mm_t(S["proj"][l], W["qkv"][l])
    tick()

    def last(rows, slot):
        gn = S["gn"][rows, :]
        n = S["n_a"][l, rows, :].astype(f32)
        inv = S["inv"][rows, l : l + 1]
        add_mod(S, l, slot, 0, gn)
        add_mod(S, l, slot, 1, gn * n)
        g = S["h"][rows, :] + norm_pull((1.0 + mod_part(S, l, slot, 1)) * gn, n, inv)
        if l == 0:
            S["glat_out"][rows, :] = g.astype(bf16)
        else:
            S["h"][rows, :] = g

    row_chunks(last)
    gm = S["gmod"][l]
    hi = gm.astype(bf16)
    lo = (gm - hi.astype(f32)).astype(bf16)
    silu = S["silu"][...]
    eight = jnp.ones((8, 8), bf16)
    G["b_ada"][...] = mm(eight, hi) + mm(eight, lo)
    G["ada"][...] = (t_mm(silu, hi) + t_mm(silu, lo)).astype(bf16)


def backward_silu(l, W, S):
    gm = S["gmod"][l]
    hi = gm.astype(bf16)
    lo = (gm - hi.astype(f32)).astype(bf16)
    w = W["ada"][l]
    grad_silu = mm_t(hi, w) + mm_t(lo, w)
    if l == LAYERS - 1:
        S["gsilu"][...] = grad_silu
    else:
        S["gsilu"][...] += grad_silu


SCRATCH = dict(
    cond=((8, D), f32),
    live=((8, D), f32),
    mod=((LAYERS, 8, 6 * D), f32),
    gmod=((LAYERS, 8, 6 * D), f32),
    silu=((8, D), bf16),
    gsilu=((8, D), f32),
    h=((ROWS, D), f32),
    go=((ROWS, D), bf16),
    gn=((ROWS, D), f32),
    n_a=((LAYERS, ROWS, D), bf16),
    n_m=((LAYERS, ROWS, D), bf16),
    inv=((ROWS, 128), f32),
    normed=((LAYERS, ROWS, D), bf16),
    normed_m=((LAYERS, ROWS, D), bf16),
    proj=((LAYERS, ROWS, 3 * D), bf16),
    prob=((LAYERS, SLOTS * HEADS, LEN, LEN), bf16),
    att=((LAYERS, ROWS, D), bf16),
    branch=((LAYERS, ROWS, D), bf16),
    activated=((LAYERS, ROWS, FF), bf16),
    slope=((LAYERS, ROWS, FF), bf16),
    output=((LAYERS, ROWS, D), bf16),
)
WEIGHTS = dict(
    ada=((LAYERS, D, 6 * D), bf16),
    b_ada=((LAYERS, 1, 6 * D), f32),
    qkv=((LAYERS, D, 3 * D), bf16),
    b_qv=((LAYERS, 1, 2 * D), f32),
    proj=((LAYERS, D, D), bf16),
    b_proj=((LAYERS, 1, D), f32),
    fc1=((LAYERS, D, FF), bf16),
    b_fc1=((LAYERS, 1, FF), f32),
    fc2=((LAYERS, FF, D), bf16),
    b_fc2=((LAYERS, 1, D), f32),
)
GRADS = dict(
    ada=((D, 6 * D), bf16),
    b_ada=((8, 6 * D), f32),
    qkv=((D, 3 * D), bf16),
    b_qv=((8, 2 * D), f32),
    proj=((D, D), bf16),
    b_proj=((8, D), f32),
    b_fc1=((8, FF), f32),
    fc2=((FF, D), bf16),
    b_fc2=((8, D), f32),
)

MESH = pl.DeviceIdType.MESH
STRIDE = (2, 8, 32)
ORDER = ((0, 1, 2), (1, 2, 0), (2, 0, 1))
PARTS = 3
SIDE = 4
DEVS = 128
UNITS = 4
BLOCK = 32
HALF = BLOCK // 2
GROUPS = DEVS // 16
WHOLE = (UNITS, PARTS, 2, SIDE, SIDE, SIDE, BLOCK, 128)


class Place:
    def __init__(self):
        me = lax.axis_index("dp")
        self.core = me % 2
        self.at = ((me // 2) % 4, (me // 8) % 4, me // 32)
        self.me = me
        self.sibling = me + 1 - 2 * self.core

    def beside(self, axis, step):
        here = self.at[axis]
        return self.me + ((here + step) % 4 - here) * STRIDE[axis]

    def turn(self, p, phase, step):
        return (self.at[ORDER[p][phase]] + step) % 4


def greet(place):
    barrier = pltpu.get_barrier_semaphore()
    for axis in range(3):
        for step in (1, 2, 3):
            pl.semaphore_signal(
                barrier, inc=1, device_id=(place.beside(axis, step),), device_id_type=MESH
            )
    pl.semaphore_signal(barrier, inc=1, device_id=(place.sibling,), device_id_type=MESH)
    pl.semaphore_wait(barrier, 10)


def slab(G, place, u, p, core, phase, j, half=None):
    i2 = place.at[ORDER[p][2]]
    i1 = place.at[ORDER[p][1]]
    rows = slice(None) if half is None else slice(half * HALF, half * HALF + HALF)
    if phase == 0:
        return G.at[u, p, core, i2, i1, j, rows, :]
    if phase == 1:
        return G.at[u, p, core, i2, j, :, rows, :]
    return G.at[u, p, core, j, :, :, rows, :]


def remote(src, dst, send, recv, target):
    return pltpu.make_async_remote_copy(
        src_ref=src,
        dst_ref=dst,
        send_sem=send,
        recv_sem=recv,
        device_id=(target,),
        device_id_type=MESH,
    )


DIRECT = (2, 1, 3)
RING_OUT = ((0, None, 1), (0, None, 3), (3, 0, 1), (1, 1, 3))
RING_IN = ((3, None, 3), (1, None, 1), (2, 0, 3), (2, 1, 1))


class Gather:
    def __init__(self, place, G, sems):
        self.place, self.G = place, G
        self.send, self.recv, self.send_pair, self.recv_pair = sems

    def copy(self, u, p, phase, kind, arriving=False):
        place = self.place
        axis = ORDER[p][phase]
        half = None
        if phase < 2:
            step = DIRECT[kind]
            other = 4 - step if arriving else step
            j = 4 - step if arriving else 0
        else:
            j, half, other = (RING_IN if arriving else RING_OUT)[kind]
        ref = slab(self.G, place, u, p, place.core, phase, place.turn(p, phase, j), half)
        return remote(
            ref,
            ref,
            self.send.at[u, p, phase, kind],
            self.recv.at[u, p, phase, kind],
            place.beside(axis, other),
        )

    def pair(self, u, p, kind, mine):
        place = self.place
        step = (0, 3, 1, 2)[kind]
        core = place.core if mine else 1 - place.core
        ref = slab(self.G, place, u, p, core, 2, place.turn(p, 2, step))
        return remote(
            ref, ref, self.send_pair.at[u, p, kind], self.recv_pair.at[u, p, kind], place.sibling
        )

    def first(self, u, p, phase):
        for kind in range(3 if phase < 2 else 2):
            self.copy(u, p, phase, kind).start()

    def direct(self, u, phase):
        for p in range(PARTS):
            for kind in (1, 2, 0):
                self.copy(u, p, phase, kind, True).wait_recv()
            self.first(u, p, phase + 1)
            if phase == 1:
                self.pair(u, p, 0, True).start()

    def forward(self, u):
        for p in range(PARTS):
            for kind in (0, 1):
                self.copy(u, p, 2, kind, True).wait_recv()
                self.copy(u, p, 2, 2 + kind).start()
                self.pair(u, p, 1 + kind, True).start()

    def close(self, u):
        for p in range(PARTS):
            for kind in (2, 3):
                self.copy(u, p, 2, kind, True).wait_recv()
            self.pair(u, p, 3, True).start()

    def wait_pair(self, u):
        for p in range(PARTS):
            for kind in range(4):
                self.pair(u, p, kind, False).wait_recv()

    def wait_sends(self, u):
        for p in range(PARTS):
            for phase in range(3):
                for kind in range(3 if phase < 2 else 4):
                    self.copy(u, p, phase, kind).wait_send()
            for kind in range(4):
                self.pair(u, p, kind, True).wait_send()


class Scatter:
    def __init__(self, place, G, pair_in, half_in, full_in, sems):
        self.place, self.G = place, G
        self.pair_in, self.half_in, self.full_in = pair_in, half_in, full_in
        self.send, self.recv, self.send_pair, self.recv_pair = sems

    def pair(self, u, p):
        place = self.place
        return remote(
            self.G.at[u, p, 1 - place.core],
            self.pair_in.at[u, p],
            self.send_pair.at[u, p],
            self.recv_pair.at[u, p],
            place.sibling,
        )

    def start(self, u):
        for p in range(PARTS):
            self.pair(u, p).start()

    def copy(self, u, p, phase, kind):
        place = self.place
        axis = ORDER[p][phase]
        half = None
        if phase < 2:
            j = other = DIRECT[kind]
            dst = self.full_in[phase].at[u, p, kind]
        else:
            j, half, other = ((2, 0, 1), (2, 1, 3), (1, None, 1), (3, None, 3))[kind]
            dst = (self.half_in if kind < 2 else self.full_in[2]).at[u, p, kind % 2]
        src = slab(self.G, place, u, p, place.core, phase, place.turn(p, phase, j), half)
        return remote(
            src,
            dst,
            self.send.at[u, p, phase, kind],
            self.recv.at[u, p, phase, kind],
            place.beside(axis, other),
        )

    def first(self, u, p, phase):
        for kind in range(3 if phase < 2 else 2):
            self.copy(u, p, phase, kind).start()

    def add_pair(self, u):
        place = self.place
        for p in range(PARTS):
            self.pair(u, p).wait_recv()
            for step in (2, 1, 3, 0):
                j = place.turn(p, 2, step)
                target = self.G.at[u, p, place.core, j]
                source = self.pair_in.at[u, p, j]

                @pl.loop(0, SIDE)
                def _(k):
                    target[k] = (target[k].astype(f32) + source[k].astype(f32)).astype(bf16)

                if step == 2:
                    self.first(u, p, 2)

    def forward(self, u):
        place = self.place
        for p in range(PARTS):
            for kind in (0, 1):
                self.copy(u, p, 2, kind).wait_recv()
                target = slab(
                    self.G, place, u, p, place.core, 2, place.turn(p, 2, 1 + 2 * kind), kind
                )
                source = self.half_in.at[u, p, kind]

                @pl.loop(0, SIDE)
                def _(k):
                    target[k] = (target[k].astype(f32) + source[k].astype(f32)).astype(bf16)

                self.copy(u, p, 2, 2 + kind).start()

    def close(self, u):
        place = self.place
        for p in range(PARTS):
            for kind in (2, 3):
                self.copy(u, p, 2, kind).wait_recv()
            target = slab(self.G, place, u, p, place.core, 2, place.turn(p, 2, 0))
            left, right = self.full_in[2].at[u, p, 0], self.full_in[2].at[u, p, 1]

            @pl.loop(0, SIDE)
            def _(k):
                target[k] = (
                    target[k].astype(f32) + (left[k].astype(f32) + right[k].astype(f32))
                ).astype(bf16)

            self.first(u, p, 1)

    def direct(self, u, phase, out_ref):
        place = self.place
        for p in range(PARTS):
            for kind in (1, 2, 0):
                self.copy(u, p, phase, kind).wait_recv()
            target = slab(self.G, place, u, p, place.core, phase, place.turn(p, phase, 0))
            a, b, c = (self.full_in[phase][u, p, kind].astype(f32) for kind in range(3))
            total = (target[...].astype(f32) + a) + (b + c)
            if phase == 0:
                out_ref[u, p] = total
            else:
                target[...] = total.astype(bf16)
                self.first(u, p, 0)

    def events(self, u, out_ref):
        return [
            lambda: self.add_pair(u),
            lambda: self.forward(u),
            lambda: self.close(u),
            lambda: self.direct(u, 1, out_ref),
            lambda: self.direct(u, 0, out_ref),
        ]

    def wait_sends(self, u):
        for p in range(PARTS):
            self.pair(u, p).wait_send()
            for phase in range(3):
                for kind in range(3 if phase < 2 else 4):
                    self.copy(u, p, phase, kind).wait_send()


def tile_refs(G, u, group, tile):
    z = group // 2
    for p in range(PARTS):
        for i in range(16):
            y_low, x, core = i // 8, (i // 2) % 4, i % 2
            at = (x, (group % 2) * 2 + y_low, z)
            o = ORDER[p]
            yield p, i, G.at[
                u, p, core, at[o[2]], at[o[1]], at[o[0]], tile * 16 : tile * 16 + 16, :
            ]


def pick(G, u, group, tile):
    parts = [[], [], []]
    for p, i, ref in tile_refs(G, u, group, tile):
        parts[p].append(ref[...])
    return jnp.concatenate([jnp.concatenate(part, axis=0) for part in parts], axis=1)


def put(G, u, group, tile, value):
    for p, i, ref in tile_refs(G, u, group, tile):
        ref[...] = value[i * 16 : i * 16 + 16, p * 128 : p * 128 + 128]


ATTENTION_TILES = (
    tuple(("ada", k) for k in range(5)),
    (("ada", 5), ("qkv", 0), ("qkv", 1), ("qkv", 2), ("proj", 0)),
)
MLP_TILE = (("fc1", 0), ("fc1", 1), ("fc1", 2), ("fc1", 3))
BIASES = (
    (("b_ada", 0, 18), ("b_qv", 18, 6), ("b_proj", 24, 3)),
    (("b_fc1", 0, 12), ("b_fc2", 12, 3)),
)


def spread(at, width, start):
    n = lax.broadcasted_iota(jnp.int32, (1, D), 1).astype(f32) + float(start)
    owner = jnp.floor((n + 0.5) * (1.0 / width))
    lane = (n - width * owner) + float(at)
    row = lax.broadcasted_iota(jnp.int32, (DEVS, D), 0).astype(f32)
    return row == owner, row == lane


def unpack_bias(u, W, bias_ref):
    ones = jnp.ones((8, DEVS), bf16)
    rows = bias_ref[...]
    for name, at, width in BIASES[u % 2]:
        for start in range(0, DEVS * width, D):
            owner, lane = spread(at, width, start)
            value = mm(rows, jnp.where(lane, 1.0, 0.0).astype(bf16))
            value = mm(ones, jnp.where(owner, value, 0.0).astype(bf16))
            W[name][u // 2, :, start : start + D] = value[0:1, :]


def pack_bias(u, grads, bias_ref):
    total = jnp.zeros((DEVS, DEVS), f32)
    for name, at, width in BIASES[u % 2]:
        for start in range(0, DEVS * width, D):
            owner, lane = spread(at, width, start)
            value = jnp.where(owner, grads[name][0:1, start : start + D], 0.0).astype(bf16)
            total = total + mm_t(value, jnp.where(lane, 1.0, 0.0).astype(bf16))
    bias_ref[...] = total.astype(bf16)


def unpack_unit(u, G, perm, W, bias_ref):
    l = u // 2

    @pl.loop(0, GROUPS)
    def _(group):
        rows = pl.ds(pl.multiple_of(group * 48, 16), 48)
        devs = pl.ds(pl.multiple_of(group * 16, 16), 16)
        tiles = ATTENTION_TILES if u % 2 == 0 else (MLP_TILE,)
        for tile, members in enumerate(tiles):
            out = mm(perm[0], pick(G, u, group, tile)).astype(bf16)
            for k, (name, block) in enumerate(members):
                W[name][l, rows, block * D : (block + 1) * D] = out[k * 48 : k * 48 + 48, :]
            if tile == len(tiles) - 1:
                bias_ref[devs, :] = out[240:256, 0:128]
        if u % 2 == 1:
            out = mm(perm[1], pick(G, u, group, 1)).astype(bf16)
            W["fc2"][l, pl.ds(pl.multiple_of(group * 192, 16), 192), :] = out[0:192, :]

    unpack_bias(u, W, bias_ref)


def pack_unit(u, G, perm, grads, bias_ref):
    pack_bias(u, grads, bias_ref)

    def zero(n, width=D):
        return jnp.zeros((n, width), bf16)

    @pl.loop(0, GROUPS)
    def _(group):
        rows = pl.ds(pl.multiple_of(group * 48, 16), 48)
        devs = pl.ds(pl.multiple_of(group * 16, 16), 16)
        tiles = ATTENTION_TILES if u % 2 == 0 else (MLP_TILE,)
        for tile, members in enumerate(tiles):
            pieces = [grads[name][rows, block * D : (block + 1) * D] for name, block in members]
            if len(pieces) < 5:
                pieces.append(zero(48))
            if tile == len(tiles) - 1:
                pieces.append(jnp.concatenate([bias_ref[devs, :], zero(16, D - 128)], axis=1))
            else:
                pieces.append(zero(16))
            put(G, u, group, tile, t_mm(perm[0], jnp.concatenate(pieces, axis=0)).astype(bf16))
        if u % 2 == 1:
            piece = grads["fc2"][pl.ds(pl.multiple_of(group * 192, 16), 192), :]
            value = jnp.concatenate([piece, zero(64)], axis=0)
            put(G, u, group, 1, t_mm(perm[1], value).astype(bf16))


def permutations():
    out = np.zeros((2, 256, 256), np.float32)
    for o in range(256):
        if o < 240:
            k, rest = divmod(o, 48)
            dev, r = divmod(rest, 3)
            out[0, o, dev * 16 + k * 3 + r] = 1
        else:
            out[0, o, (o - 240) * 16 + 15] = 1
        if o < 192:
            dev, r = divmod(o, 12)
            out[1, o, dev * 16 + r] = 1
        else:
            dev, r = divmod(o - 192, 4)
            out[1, o, dev * 16 + 12 + r] = 1
    return out


SHARDS = tuple(WEIGHTS)


def pack_own(place, own, G, rows_ref, line_ref):
    lines = []
    for members in BIASES:
        line = None
        for name, at, width in members:
            line_ref[...] = jnp.zeros((8, 128), f32)
            line_ref[0:LAYERS, 0:width] = own[name][...].astype(f32)
            piece = line_ref[...]
            if at:
                piece = pltpu.roll(piece, at, 1)
            line = piece if line is None else line + piece
        lines.append(line)
    for u in range(UNITS):
        l = u // 2
        rows_ref[...] = jnp.zeros((BLOCK, D), f32)
        if u % 2 == 0:
            for tile, members in enumerate(ATTENTION_TILES):
                for k, (name, block) in enumerate(members):
                    row = tile * 16 + k * 3
                    rows_ref[row : row + 3, :] = own[name][
                        l, :, block * D : (block + 1) * D
                    ].astype(f32)
            rows_ref[31:32, 0:128] = lines[0][l : l + 1, :]
        else:
            for k, (name, block) in enumerate(MLP_TILE):
                rows_ref[k * 3 : k * 3 + 3, :] = own[name][
                    l, :, block * D : (block + 1) * D
                ].astype(f32)
            rows_ref[16:28, :] = own["fc2"][l].astype(f32)
            rows_ref[15:16, 0:128] = lines[1][l : l + 1, :]
        for p in range(PARTS):
            ref = slab(G, place, u, p, place.core, 0, place.turn(p, 0, 0))
            ref[...] = rows_ref[:, p * 128 : p * 128 + 128].astype(bf16)


def step_kernel(*refs):
    lat, cond, cot, table, counts = refs[:5]
    own = dict(zip(SHARDS, refs[5:15]))
    perm = refs[15]
    act, glat, gcond, shard = refs[16:20]
    at = 20
    G, pair_in, half_in, f0, f1, f2, bias_ref, rows_ref, line_ref = refs[at : at + 9]
    at += 9
    gather_sems, scatter_sems = refs[at : at + 4], refs[at + 4 : at + 8]
    at += 8
    W = dict(zip(WEIGHTS, refs[at : at + 10]))
    grads = dict(zip(GRADS, refs[at + 10 : at + 19]))
    grads["fc1"] = grads["ada"].at[:, 0:FF]
    S = dict(zip(SCRATCH, refs[at + 19 :]))
    S.update(lat=lat, cot=cot, act_out=act, glat_out=glat)

    place = Place()
    pack_own(place, own, G, rows_ref, line_ref)
    greet(place)
    gather = Gather(place, G, gather_sems)
    for u in range(UNITS):
        for p in range(PARTS):
            gather.first(u, p, 0)

    S["cond"][...] = jnp.zeros((8, D), f32)
    S["cond"][0:SLOTS, :] = cond[...].astype(f32)
    c = S["cond"][...]
    S["silu"][...] = (c / (1.0 + jnp.exp(-c))).astype(bf16)
    S["live"][...] = jnp.zeros((8, D), f32)
    for slot in range(SLOTS):
        alive = jnp.zeros((), f32)
        for position in range(SLOTS):
            chosen = (table[0, position] == slot) & (position < counts[0])
            alive = alive + jnp.where(chosen, 1.0, 0.0)
        S["live"][slot : slot + 1, :] = jnp.full((1, D), alive, f32)

    queue = []

    def tick():
        if queue:
            queue.pop(0)()

    def drain():
        while queue:
            queue.pop(0)()

    for u in range(UNITS):
        gather.direct(u, 0)
    gather.direct(0, 1)
    gather.direct(1, 1)
    gather.forward(0)
    gather.close(0)
    gather.direct(2, 1)
    gather.wait_pair(0)
    unpack_unit(0, G, perm, W, bias_ref)
    gather.forward(1)
    queue += [
        lambda: gather.close(1),
        lambda: gather.direct(3, 1),
        lambda: gather.forward(2),
        lambda: gather.close(2),
    ]
    forward_attention(0, W, S, tick)
    drain()
    gather.wait_pair(1)
    unpack_unit(1, G, perm, W, bias_ref)
    queue += [lambda: gather.forward(3), lambda: gather.close(3)]
    forward_mlp(0, W, S, tick)
    drain()
    gather.wait_pair(2)
    unpack_unit(2, G, perm, W, bias_ref)
    forward_attention(1, W, S, tick)
    gather.wait_pair(3)
    unpack_unit(3, G, perm, W, bias_ref)
    forward_mlp(1, W, S, tick)
    for u in range(UNITS):
        gather.wait_sends(u)

    scatter = Scatter(place, G, pair_in, half_in, (f0, f1, f2), scatter_sems)
    for l in reversed(range(LAYERS)):
        backward_mlp(l, W, S, grads, tick)
        pack_unit(2 * l + 1, G, perm, grads, bias_ref)
        scatter.start(2 * l + 1)
        queue += scatter.events(2 * l + 1, shard)
        backward_middle(l, W, S, grads, tick)
        backward_end(l, W, S, grads, tick)
        pack_unit(2 * l, G, perm, grads, bias_ref)
        scatter.start(2 * l)
        if l == 0:
            rest, queue[:] = list(queue), []
            mine = scatter.events(0, shard)
            for k in range(max(len(rest), len(mine))):
                queue += rest[k : k + 1] + mine[k : k + 1]
        else:
            queue += scatter.events(2 * l, shard)
        backward_silu(l, W, S)
    sig = 1.0 / (1.0 + jnp.exp(-c))
    gcond[...] = S["gsilu"][...] * (sig * (1.0 + c * (1.0 - sig)))
    drain()
    for u in range(UNITS):
        scatter.wait_sends(u)


def run_step(args, perm):
    vmem = pl.BlockSpec(memory_space=pltpu.VMEM)
    smem = pl.BlockSpec(memory_space=pltpu.SMEM)
    ring = (UNITS, PARTS, 3, 4)
    scratch = [
        pltpu.VMEM(WHOLE, bf16),
        pltpu.VMEM((UNITS, PARTS, SIDE, SIDE, SIDE, BLOCK, 128), bf16),
        pltpu.VMEM((UNITS, PARTS, 2, SIDE, SIDE, HALF, 128), bf16),
        pltpu.VMEM((UNITS, PARTS, 3, BLOCK, 128), bf16),
        pltpu.VMEM((UNITS, PARTS, 3, SIDE, BLOCK, 128), bf16),
        pltpu.VMEM((UNITS, PARTS, 2, SIDE, SIDE, BLOCK, 128), bf16),
        pltpu.VMEM((DEVS, 128), bf16),
        pltpu.VMEM((BLOCK, D), f32),
        pltpu.VMEM((8, 128), f32),
        pltpu.SemaphoreType.DMA(ring),
        pltpu.SemaphoreType.DMA(ring),
        pltpu.SemaphoreType.DMA((UNITS, PARTS, 4)),
        pltpu.SemaphoreType.DMA((UNITS, PARTS, 4)),
        pltpu.SemaphoreType.DMA(ring),
        pltpu.SemaphoreType.DMA(ring),
        pltpu.SemaphoreType.DMA((UNITS, PARTS)),
        pltpu.SemaphoreType.DMA((UNITS, PARTS)),
    ]
    for table in (WEIGHTS, GRADS, SCRATCH):
        scratch += [pltpu.VMEM(s, t) for s, t in table.values()]
    return pl.pallas_call(
        step_kernel,
        out_shape=[
            jax.ShapeDtypeStruct((ROWS, D), bf16),
            jax.ShapeDtypeStruct((ROWS, D), bf16),
            jax.ShapeDtypeStruct((8, D), f32),
            jax.ShapeDtypeStruct((UNITS, PARTS, BLOCK, 128), f32),
        ],
        in_specs=[vmem] * 3 + [smem] * 2 + [vmem] * 11,
        out_specs=[vmem] * 4,
        scratch_shapes=scratch,
        compiler_params=pltpu.CompilerParams(
            collective_id=0, has_side_effects=True, vmem_limit_bytes=VMEM_BYTES
        ),
    )(*args, perm)


def finish_kernel(act_in, glat_in, gcond_in, shard, act, glat, gcond, *outs):
    act[...] = act_in[...]
    glat[...] = glat_in[...]
    gcond[...] = gcond_in[0:SLOTS, :]
    out = dict(zip(SHARDS, outs))
    for u in range(UNITS):
        l = u // 2
        tiles = ATTENTION_TILES if u % 2 == 0 else (MLP_TILE,)
        for p in range(PARTS):
            for tile, members in enumerate(tiles):
                for k, (name, block) in enumerate(members):
                    row = tile * 16 + k * 3
                    lanes = slice(block * D + p * 128, block * D + p * 128 + 128)
                    out[name][l, :, lanes] = shard[u, p, row : row + 3, :]
            if u % 2 == 1:
                out["fc2"][l, :, p * 128 : p * 128 + 128] = shard[u, p, 16:28, :]
        top = 24 if u % 2 == 0 else 8
        for name, at, width in BIASES[u % 2]:
            piece = shard[u, 0, top : top + 8, :]
            if at:
                piece = pltpu.roll(piece, 128 - at, 1)
            out[name][l : l + 1, :] = piece[7:8, 0:width]


def finish(act, glat, gcond, shard, shapes):
    vmem = pl.BlockSpec(memory_space=pltpu.VMEM)
    outs = [act, glat, jax.ShapeDtypeStruct((SLOTS, D), f32)]
    outs = [jax.ShapeDtypeStruct(o.shape, o.dtype) for o in outs]
    outs += [jax.ShapeDtypeStruct(s, f32) for s in shapes]
    return pl.pallas_call(
        finish_kernel,
        out_shape=outs,
        in_specs=[vmem] * 4,
        out_specs=[vmem] * len(outs),
    )(act, glat, gcond, shard)


def body(latents, condition, cotangent, slot_table, counts, *weights):
    perm = jnp.asarray(permutations(), bf16)
    args = (latents.reshape(ROWS, D), condition, cotangent.reshape(ROWS, D), slot_table, counts)
    result = run_step(args + weights, perm)
    act, glat, *rest = finish(*result, [w.shape for w in weights])
    return (act.reshape(SLOTS, LEN, D), glat.reshape(SLOTS, LEN, D), *rest)


def solution(mesh):
    split0 = (P("dp", None, None), P("dp", None), P("dp", None, None), P("dp", None), P("dp"))
    params = (P(None, "dp", None), P(None, "dp")) * 5
    outs = (P("dp", None, None), P("dp", None, None), P("dp", None)) + params
    return jax.shard_map(body, mesh=mesh, in_specs=split0 + params, out_specs=outs, check_vma=False)
```

```python
import functools
import jax
import jax.numpy as jnp
from jax import lax
from jax.experimental import pallas as pl
from jax.experimental.pallas import tpu as pltpu
from jax.sharding import PartitionSpec as P
import numpy as np

f32 = jnp.float32
bf16 = jnp.bfloat16
D = 384
HEADS = 6
FF = 1536
LAYERS = 2
LEN = 256
SLOTS = 2
ROWS = SLOTS * LEN
CHUNK = 64
STEPS = ROWS // CHUNK
EPS = 1e-06
GELU = 0.7978845608028654
VMEM_BYTES = 65280 * 1024


def mm(a, b):
    return lax.dot_general(a, b, (((1,), (0,)), ((), ())), preferred_element_type=f32)


def mm_t(a, b):
    return lax.dot_general(a, b, (((1,), (1,)), ((), ())), preferred_element_type=f32)


def t_mm(a, b):
    return lax.dot_general(a, b, (((0,), (0,)), ((), ())), preferred_element_type=f32)


def row_chunks(step):
    @pl.loop(0, STEPS, unroll=2)
    def _(i):
        rows = pl.ds(pl.multiple_of(i * CHUNK, CHUNK), CHUNK)
        slot = i // (STEPS // SLOTS)
        step(rows, slot)


def norm_parts(x):
    mean = jnp.mean(x, axis=-1, keepdims=True)
    centred = x - mean
    var = jnp.mean(centred * centred, axis=-1, keepdims=True)
    inv = lax.rsqrt(var + EPS)
    return centred * inv, inv


def norm_pull(u, n, inv):
    mean_u = jnp.mean(u, axis=-1, keepdims=True)
    mean_un = jnp.mean(u * n, axis=-1, keepdims=True)
    return inv * (u - mean_u - n * mean_un)


def keep_half(x, odd):
    lane = lax.broadcasted_iota(jnp.int32, (1, x.shape[1]), 1)
    mask = (lane >= 64) if odd else (lane < 64)
    return jnp.where(mask, x, jnp.zeros_like(x))


def keep_inv(S, rows, k, inv):
    lane = lax.broadcasted_iota(jnp.int32, (CHUNK, 128), 1)
    S["inv"][rows, :] = jnp.where(lane == k, inv, S["inv"][rows, :])


def mod_part(S, l, slot, k):
    return S["mod"][l, pl.ds(slot, 1), k * D : (k + 1) * D]


def norm_stream(l, S, rows):
    x = (S["lat"] if l == 0 else S["h"])[rows, :].astype(f32)
    n, inv = norm_parts(x)
    S["n_a"][l, rows, :] = n.astype(bf16)
    keep_inv(S, rows, l, inv)
    return n


def norm_first(S):
    def step(rows, slot):
        S["gn"][rows, :] = norm_stream(0, S, rows)

    row_chunks(step)


def forward_attention(l, W, S, tick):
    S["mod"][l] = mm(S["silu"][...], W["ada"][l]) + W["b_ada"][l]

    def prep(rows, slot):
        n = S["gn"][rows, :] if l == 0 else norm_stream(l, S, rows)
        S["normed"][l, rows, :] = (
            n * (1.0 + mod_part(S, l, slot, 1)) + mod_part(S, l, slot, 0)
        ).astype(bf16)

    row_chunks(prep)
    tick()
    for k in range(3):
        cols = slice(k * D, (k + 1) * D)
        out = mm(S["normed"][l], W["qkv"][l, :, cols])
        if k != 1:
            b = W["b_qv"][l, :, 0:D] if k == 0 else W["b_qv"][l, :, D:]
            out = out + b
        S["proj"][l, :, cols] = out.astype(bf16)
    tick()
    for slot in range(SLOTS):
        rows = slice(slot * LEN, slot * LEN + LEN)
        for pair in range(3):
            lanes = slice(pair * 128, pair * 128 + 128)
            q = (S["proj"][l, rows, lanes].astype(f32) * 0.125).astype(bf16)
            k = S["proj"][l, rows, D + pair * 128 : D + pair * 128 + 128]
            v = S["proj"][l, rows, 2 * D + pair * 128 : 2 * D + pair * 128 + 128]
            att = None
            for odd in range(2):
                s = mm_t(keep_half(q, odd), k)
                e = jnp.exp(s - jnp.max(s, axis=-1, keepdims=True))
                p = (e * (1.0 / jnp.sum(e, axis=-1, keepdims=True))).astype(bf16)
                S["prob"][l, slot * HEADS + pair * 2 + odd] = p
                term = mm(p, keep_half(v, odd))
                att = term if att is None else att + term
            S["att"][l, rows, lanes] = att.astype(bf16)
        tick()
    S["gn"][...] = mm(S["att"][l], W["proj"][l]) + W["b_proj"][l]
    tick()


def forward_mlp(l, W, S, tick):
    def middle(rows, slot):
        x = (S["lat"] if l == 0 else S["h"])[rows, :].astype(f32)
        branch = S["gn"][rows, :]
        S["branch"][l, rows, :] = branch.astype(bf16)
        m = x + mod_part(S, l, slot, 2) * branch
        S["h"][rows, :] = m
        n, inv = norm_parts(m)
        S["n_m"][l, rows, :] = n.astype(bf16)
        keep_inv(S, rows, LAYERS + l, inv)
        S["normed_m"][l, rows, :] = (
            n * (1.0 + mod_part(S, l, slot, 4)) + mod_part(S, l, slot, 3)
        ).astype(bf16)

    row_chunks(middle)
    tick()
    for part in range(2):

        @pl.loop(0, FF // 512, unroll=True)
        def _(j):
            cols = pl.ds(pl.multiple_of(part * (FF // 2) + j * 256, 256), 256)
            x = mm(S["normed_m"][l], W["fc1"][l, :, cols]) + W["b_fc1"][l, :, cols]
            x2 = x * x
            t = jnp.tanh(GELU * (x + 0.044715 * (x2 * x)))
            half = 0.5 * (1.0 + t)
            S["activated"][l, :, cols] = (x * half).astype(bf16)
            slope = half + 0.5 * x * (1.0 - t * t) * (GELU * (1.0 + 3 * 0.044715 * x2))
            S["slope"][l, :, cols] = slope.astype(bf16)

        tick()
    S["gn"][...] = mm(S["activated"][l], W["fc2"][l]) + W["b_fc2"][l]

    def finish(rows, slot):
        output = S["gn"][rows, :]
        S["output"][l, rows, :] = output.astype(bf16)
        r = S["h"][rows, :] + mod_part(S, l, slot, 5) * output
        if l == LAYERS - 1:
            S["act_out"][rows, :] = (r * S["live"][pl.ds(slot, 1), :]).astype(bf16)
        else:
            S["h"][rows, :] = r

    row_chunks(finish)
    tick()


def add_mod(S, l, slot, k, value):
    cols = slice(k * D, (k + 1) * D)
    S["gmod"][l, pl.ds(slot, 1), cols] += jnp.sum(value, axis=0, keepdims=True)


def backward_mlp(l, W, S, G, tick):
    ones = jnp.ones((8, ROWS), bf16)
    S["gmod"][l] = jnp.zeros((8, 6 * D), f32)

    def start(rows, slot):
        if l == LAYERS - 1:
            g = S["cot"][rows, :].astype(f32) * S["live"][pl.ds(slot, 1), :]
            S["h"][rows, :] = g
        else:
            g = S["h"][rows, :]
        add_mod(S, l, slot, 5, g * S["output"][l, rows, :].astype(f32))
        S["go"][rows, :] = (mod_part(S, l, slot, 5) * g).astype(bf16)

    row_chunks(start)
    go = S["go"]
    G["b_fc2"][...] = mm(ones, go[...])[0:1]
    for part in range(2):

        @pl.loop(0, FF // 512, unroll=True)
        def _(j):
            cols = pl.ds(pl.multiple_of(part * (FF // 2) + j * 256, 256), 256)
            gh = mm_t(go[...], W["fc2"][l, cols, :]) * S["slope"][l, :, cols].astype(f32)
            gh = gh.astype(bf16)
            G["fc2"][cols, :] = t_mm(S["activated"][l, :, cols], go[...]).astype(bf16)
            S["activated"][l, :, cols] = gh
            G["fc1"][:, cols] = t_mm(S["normed_m"][l], gh).astype(bf16)
            G["b_fc1"][:, cols] = mm(ones, gh)[0:1]

    tick()


def backward_middle(l, W, S, G, tick):
    ones = jnp.ones((8, ROWS), bf16)
    go = S["go"]
    S["gn"][...] = mm_t(S["activated"][l], W["fc1"][l])

    def mid(rows, slot):
        gn = S["gn"][rows, :]
        n = S["n_m"][l, rows, :].astype(f32)
        inv = S["inv"][rows, LAYERS + l : LAYERS + l + 1]
        add_mod(S, l, slot, 3, gn)
        add_mod(S, l, slot, 4, gn * n)
        gm = S["h"][rows, :] + norm_pull((1.0 + mod_part(S, l, slot, 4)) * gn, n, inv)
        S["h"][rows, :] = gm
        add_mod(S, l, slot, 2, gm * S["branch"][l, rows, :].astype(f32))
        S["go"][rows, :] = (mod_part(S, l, slot, 2) * gm).astype(bf16)

    row_chunks(mid)
    G["b_proj"][...] = mm(ones, go[...])[0:1]
    G["proj"][...] = t_mm(S["att"][l], go[...]).astype(bf16)
    S["att"][l] = mm_t(go[...], W["proj"][l]).astype(bf16)
    tick()
    for slot in range(SLOTS):
        rows = slice(slot * LEN, slot * LEN + LEN)
        for pair in range(3):
            lanes = slice(pair * 128, pair * 128 + 128)
            kl = slice(D + pair * 128, D + pair * 128 + 128)
            vl = slice(2 * D + pair * 128, 2 * D + pair * 128 + 128)
            q = S["proj"][l, rows, lanes]
            k = S["proj"][l, rows, kl]
            v = S["proj"][l, rows, vl]
            ga = S["att"][l, rows, lanes]
            gq = gk = gv = None
            for odd in range(2):
                low = S["prob"][l, slot * HEADS + pair * 2 + odd]
                p = low.astype(f32)
                ga_h = keep_half(ga, odd)
                gp = mm_t(ga_h, v)
                dot = jnp.sum(p * gp, axis=-1, keepdims=True)
                gs = (p * (gp - dot)).astype(bf16)
                tv = t_mm(low, ga_h)
                tq = mm(gs, keep_half(k, odd))
                tk = t_mm(gs, keep_half(q, odd))
                gv = tv if gv is None else gv + tv
                gq = tq if gq is None else gq + tq
                gk = tk if gk is None else gk + tk
            S["proj"][l, rows, lanes] = (gq * 0.125).astype(bf16)
            S["proj"][l, rows, kl] = (gk * 0.125).astype(bf16)
            S["proj"][l, rows, vl] = gv.astype(bf16)
        tick()


def backward_end(l, W, S, G, tick):
    ones = jnp.ones((8, ROWS), bf16)
    for k in range(3):
        cols = slice(k * D, (k + 1) * D)
        gpk = S["proj"][l, :, cols]
        G["qkv"][:, cols] = t_mm(S["normed"][l], gpk).astype(bf16)
        if k != 1:
            G["b_qv"][:, (k // 2) * D : (k // 2 + 1) * D] = mm(ones, gpk)[0:1]
    S["gn"][...] = mm_t(S["proj"][l], W["qkv"][l])
    tick()

    def last(rows, slot):
        gn = S["gn"][rows, :]
        n = S["n_a"][l, rows, :].astype(f32)
        inv = S["inv"][rows, l : l + 1]
        add_mod(S, l, slot, 0, gn)
        add_mod(S, l, slot, 1, gn * n)
        g = S["h"][rows, :] + norm_pull((1.0 + mod_part(S, l, slot, 1)) * gn, n, inv)
        if l == 0:
            S["glat_out"][rows, :] = g.astype(bf16)
        else:
            S["h"][rows, :] = g

    row_chunks(last)
    gm = S["gmod"][l]
    hi = gm.astype(bf16)
    lo = (gm - hi.astype(f32)).astype(bf16)
    silu = S["silu"][...]
    eight = jnp.ones((8, 8), bf16)
    G["b_ada"][...] = (mm(eight, hi) + mm(eight, lo))[0:1]
    G["ada"][...] = (t_mm(silu, hi) + t_mm(silu, lo)).astype(bf16)


def backward_silu(l, W, S):
    gm = S["gmod"][l]
    hi = gm.astype(bf16)
    lo = (gm - hi.astype(f32)).astype(bf16)
    w = W["ada"][l]
    grad_silu = mm_t(hi, w) + mm_t(lo, w)
    if l == LAYERS - 1:
        S["gsilu"][...] = grad_silu
    else:
        S["gsilu"][...] += grad_silu


SCRATCH = dict(
    cond=((8, D), f32),
    live=((8, D), f32),
    mod=((LAYERS, 8, 6 * D), f32),
    gmod=((LAYERS, 8, 6 * D), f32),
    silu=((8, D), bf16),
    gsilu=((8, D), f32),
    h=((ROWS, D), f32),
    go=((ROWS, D), bf16),
    gn=((ROWS, D), f32),
    n_a=((LAYERS, ROWS, D), bf16),
    n_m=((LAYERS, ROWS, D), bf16),
    inv=((ROWS, 128), f32),
    normed=((LAYERS, ROWS, D), bf16),
    normed_m=((LAYERS, ROWS, D), bf16),
    proj=((LAYERS, ROWS, 3 * D), bf16),
    prob=((LAYERS, SLOTS * HEADS, LEN, LEN), bf16),
    att=((LAYERS, ROWS, D), bf16),
    branch=((LAYERS, ROWS, D), bf16),
    activated=((LAYERS, ROWS, FF), bf16),
    slope=((LAYERS, ROWS, FF), bf16),
    output=((LAYERS, ROWS, D), bf16),
)
WEIGHTS = dict(
    ada=((LAYERS, D, 6 * D), bf16),
    b_ada=((LAYERS, 1, 6 * D), f32),
    qkv=((LAYERS, D, 3 * D), bf16),
    b_qv=((LAYERS, 1, 2 * D), f32),
    proj=((LAYERS, D, D), bf16),
    b_proj=((LAYERS, 1, D), f32),
    fc1=((LAYERS, D, FF), bf16),
    b_fc1=((LAYERS, 1, FF), f32),
    fc2=((LAYERS, FF, D), bf16),
    b_fc2=((LAYERS, 1, D), f32),
)
GRADS = dict(
    ada=((D, 6 * D), bf16),
    b_ada=((1, 6 * D), f32),
    qkv=((D, 3 * D), bf16),
    b_qv=((1, 2 * D), f32),
    proj=((D, D), bf16),
    b_proj=((1, D), f32),
    b_fc1=((1, FF), f32),
    fc2=((FF, D), bf16),
    b_fc2=((1, D), f32),
)

MESH = pl.DeviceIdType.MESH
STRIDE = (2, 8, 32)
ORDER = ((0, 1, 2), (1, 2, 0), (2, 0, 1))
PARTS = 3
SIDE = 4
DEVS = 128
UNITS = 4
BLOCK = 32
HALF = BLOCK // 2
GROUPS = DEVS // 16
WHOLE = (UNITS, PARTS, 2, SIDE, SIDE, SIDE, BLOCK, 128)


class Place:
    def __init__(self):
        me = lax.axis_index("dp")
        self.core = me % 2
        self.at = ((me // 2) % 4, (me // 8) % 4, me // 32)
        self.me = me
        self.sibling = me + 1 - 2 * self.core

    def beside(self, axis, step):
        here = self.at[axis]
        return self.me + ((here + step) % 4 - here) * STRIDE[axis]

    def turn(self, p, phase, step):
        return (self.at[ORDER[p][phase]] + step) % 4


def greet(place, between):
    barrier = pltpu.get_barrier_semaphore()
    for axis in range(3):
        for step in (1, 2, 3):
            pl.semaphore_signal(
                barrier, inc=1, device_id=(place.beside(axis, step),), device_id_type=MESH
            )
    pl.semaphore_signal(barrier, inc=1, device_id=(place.sibling,), device_id_type=MESH)
    between()
    pl.semaphore_wait(barrier, 10)


def slab(G, place, u, p, core, phase, j, half=None):
    i2 = place.at[ORDER[p][2]]
    i1 = place.at[ORDER[p][1]]
    rows = slice(None) if half is None else slice(half * HALF, half * HALF + HALF)
    if phase == 0:
        return G.at[u, p, core, i2, i1, j, rows, :]
    if phase == 1:
        return G.at[u, p, core, i2, j, :, rows, :]
    return G.at[u, p, core, j, :, :, rows, :]


def remote(src, dst, send, recv, target):
    return pltpu.make_async_remote_copy(
        src_ref=src,
        dst_ref=dst,
        send_sem=send,
        recv_sem=recv,
        device_id=(target,),
        device_id_type=MESH,
    )


DIRECT = (2, 1, 3)
EVERY = slice(0, UNITS)
LATER = slice(1, UNITS)
RING_OUT = ((0, None, 1), (0, None, 3), (3, 0, 1), (1, 1, 3))
RING_IN = ((3, None, 3), (1, None, 1), (2, 0, 3), (2, 1, 1))


class Gather:
    def __init__(self, place, G, sems):
        self.place, self.G = place, G
        self.send, self.recv, self.send_pair, self.recv_pair = sems

    def copy(self, u, p, phase, kind, arriving=False):
        place = self.place
        s = u.start if isinstance(u, slice) else u
        axis = ORDER[p][phase]
        half = None
        if phase < 2:
            step = DIRECT[kind]
            other = 4 - step if arriving else step
            j = 4 - step if arriving else 0
        else:
            j, half, other = (RING_IN if arriving else RING_OUT)[kind]
        ref = slab(self.G, place, u, p, place.core, phase, place.turn(p, phase, j), half)
        return remote(
            ref,
            ref,
            self.send.at[s, p, phase, kind],
            self.recv.at[s, p, phase, kind],
            place.beside(axis, other),
        )

    def pair(self, u, p, kind, mine):
        place = self.place
        step = (0, 3, 1, 2)[kind]
        core = place.core if mine else 1 - place.core
        ref = slab(self.G, place, u, p, core, 2, place.turn(p, 2, step))
        return remote(
            ref, ref, self.send_pair.at[u, p, kind], self.recv_pair.at[u, p, kind], place.sibling
        )

    def first(self, u, p, phase):
        for kind in range(3 if phase < 2 else 2):
            self.copy(u, p, phase, kind).start()

    def arrive(self, u, p, phase):
        for kind in (1, 2, 0):
            self.copy(u, p, phase, kind, True).wait_recv()

    def last(self, u):
        for p in range(PARTS):
            self.first(u, p, 2)
            self.pair(u, p, 0, True).start()

    def forward(self, u):
        for p in range(PARTS):
            for kind in (0, 1):
                self.copy(u, p, 2, kind, True).wait_recv()
                self.copy(u, p, 2, 2 + kind).start()
                self.pair(u, p, 1 + kind, True).start()

    def close(self, u):
        for p in range(PARTS):
            for kind in (2, 3):
                self.copy(u, p, 2, kind, True).wait_recv()
            self.pair(u, p, 3, True).start()

    def wait_pair(self, u):
        for p in range(PARTS):
            for kind in range(4):
                self.pair(u, p, kind, False).wait_recv()

    def wait_sends(self):
        for p in range(PARTS):
            for kind in range(3):
                self.copy(EVERY, p, 0, kind).wait_send()
                self.copy(0, p, 1, kind).wait_send()
                self.copy(LATER, p, 1, kind).wait_send()
            for u in range(UNITS):
                for kind in range(4):
                    self.copy(u, p, 2, kind).wait_send()
                    self.pair(u, p, kind, True).wait_send()


class Scatter:
    def __init__(self, place, G, pair_in, full_in, sems):
        self.place, self.G = place, G
        self.pair_in, self.full_in = pair_in, full_in
        self.send, self.recv, self.send_pair, self.recv_pair = sems

    def pair(self, u, p):
        place = self.place
        return remote(
            self.G.at[u, p, 1 - place.core],
            self.pair_in.at[u, p],
            self.send_pair.at[u, p],
            self.recv_pair.at[u, p],
            place.sibling,
        )

    def start(self, u):
        for p in range(PARTS):
            self.pair(u, p).start()

    def copy(self, u, p, phase, kind):
        place = self.place
        step = DIRECT[kind]
        return remote(
            slab(self.G, place, u, p, place.core, phase, place.turn(p, phase, step)),
            self.full_in[phase].at[u, p, kind],
            self.send.at[u, p, phase, kind],
            self.recv.at[u, p, phase, kind],
            place.beside(ORDER[p][phase], step),
        )

    def first(self, u, p, phase):
        for kind in range(3):
            self.copy(u, p, phase, kind).start()

    def add_pair(self, u):
        place = self.place
        for p in range(PARTS):
            self.pair(u, p).wait_recv()
            for kind in range(4):
                j = place.turn(p, 2, (DIRECT + (0,))[kind])
                target = self.G.at[u, p, place.core, j]
                source = self.pair_in.at[u, p, j]

                @pl.loop(0, SIDE)
                def _(k):
                    target[k] = (target[k].astype(f32) + source[k].astype(f32)).astype(bf16)

                if kind < 3:
                    self.copy(u, p, 2, kind).start()

    def direct(self, u, phase, out_ref):
        place = self.place
        for p in range(PARTS):
            for kind in (1, 2, 0):
                self.copy(u, p, phase, kind).wait_recv()
            target = slab(self.G, place, u, p, place.core, phase, place.turn(p, phase, 0))
            parts = [self.full_in[phase].at[u, p, kind] for kind in range(3)]

            def total(*at):
                a, b, c = (part[at].astype(f32) for part in parts)
                return (target[at].astype(f32) + a) + (b + c)

            if phase == 0:
                out_ref[u, p] = total(slice(None))
                continue
            if phase == 1:
                target[...] = total(slice(None)).astype(bf16)
            else:

                @pl.loop(0, SIDE)
                def _(k):
                    target[k] = total(k).astype(bf16)

            self.first(u, p, phase - 1)

    def events(self, u, out_ref):
        return [
            lambda: self.add_pair(u),
            lambda: self.direct(u, 2, out_ref),
            lambda: self.direct(u, 1, out_ref),
            lambda: self.direct(u, 0, out_ref),
        ]

    def wait_sends(self, u):
        for p in range(PARTS):
            self.pair(u, p).wait_send()
            for phase in range(3):
                for kind in range(3):
                    self.copy(u, p, phase, kind).wait_send()


def tile_refs(G, u, group, tile):
    z = group // 2
    for p in range(PARTS):
        for i in range(16):
            y_low, x, core = i // 8, (i // 2) % 4, i % 2
            at = (x, (group % 2) * 2 + y_low, z)
            o = ORDER[p]
            yield p, i, G.at[
                u, p, core, at[o[2]], at[o[1]], at[o[0]], tile * 16 : tile * 16 + 16, :
            ]


def pick(G, u, group, tile):
    parts = [[], [], []]
    for p, i, ref in tile_refs(G, u, group, tile):
        parts[p].append(ref[...])
    return jnp.concatenate([jnp.concatenate(part, axis=0) for part in parts], axis=1)


def put(G, u, group, tile, value):
    for p, i, ref in tile_refs(G, u, group, tile):
        ref[...] = value[i * 16 : i * 16 + 16, p * 128 : p * 128 + 128]


ATTENTION_TILES = (
    tuple(("ada", k) for k in range(5)),
    (("ada", 5), ("qkv", 0), ("qkv", 1), ("qkv", 2), ("proj", 0)),
)
MLP_TILE = (("fc1", 0), ("fc1", 1), ("fc1", 2), ("fc1", 3))
BIASES = (
    (("b_ada", 0, 18), ("b_qv", 18, 6), ("b_proj", 24, 3)),
    (("b_fc1", 0, 12), ("b_fc2", 12, 3)),
)


def spread(at, width, start):
    n = lax.broadcasted_iota(jnp.int32, (1, D), 1).astype(f32) + float(start)
    owner = jnp.floor((n + 0.5) * (1.0 / width))
    lane = (n - width * owner) + float(at)
    row = lax.broadcasted_iota(jnp.int32, (DEVS, D), 0).astype(f32)
    return row == owner, row == lane


def unpack_bias(u, W, bias_ref):
    ones = jnp.ones((8, DEVS), bf16)
    rows = bias_ref[...]
    for name, at, width in BIASES[u % 2]:
        for start in range(0, DEVS * width, D):
            owner, lane = spread(at, width, start)
            value = mm(rows, jnp.where(lane, 1.0, 0.0).astype(bf16))
            value = mm(ones, jnp.where(owner, value, 0.0).astype(bf16))
            W[name][u // 2, :, start : start + D] = value[0:1, :]


def pack_bias(u, grads, bias_ref):
    total = jnp.zeros((DEVS, DEVS), f32)
    for name, at, width in BIASES[u % 2]:
        for start in range(0, DEVS * width, D):
            owner, lane = spread(at, width, start)
            value = jnp.where(owner, grads[name][0:1, start : start + D], 0.0).astype(bf16)
            total = total + mm_t(value, jnp.where(lane, 1.0, 0.0).astype(bf16))
    bias_ref[...] = total.astype(bf16)


def unpack_unit(u, G, perm, W, bias_ref):
    l = u // 2

    @pl.loop(0, GROUPS, unroll=4)
    def _(group):
        rows = pl.ds(pl.multiple_of(group * 48, 16), 48)
        devs = pl.ds(pl.multiple_of(group * 16, 16), 16)
        tiles = ATTENTION_TILES if u % 2 == 0 else (MLP_TILE,)
        for tile, members in enumerate(tiles):
            out = mm(perm[0], pick(G, u, group, tile)).astype(bf16)
            for k, (name, block) in enumerate(members):
                W[name][l, rows, block * D : (block + 1) * D] = out[k * 48 : k * 48 + 48, :]
            if tile == len(tiles) - 1:
                bias_ref[devs, :] = out[240:256, 0:128]
        if u % 2 == 1:
            out = mm(perm[1], pick(G, u, group, 1)).astype(bf16)
            W["fc2"][l, pl.ds(pl.multiple_of(group * 192, 16), 192), :] = out[0:192, :]

    unpack_bias(u, W, bias_ref)


def pack_unit(u, G, perm, grads, bias_ref):
    pack_bias(u, grads, bias_ref)

    def zero(n, width=D):
        return jnp.zeros((n, width), bf16)

    @pl.loop(0, GROUPS, unroll=4)
    def _(group):
        rows = pl.ds(pl.multiple_of(group * 48, 16), 48)
        devs = pl.ds(pl.multiple_of(group * 16, 16), 16)
        tiles = ATTENTION_TILES if u % 2 == 0 else (MLP_TILE,)
        for tile, members in enumerate(tiles):
            pieces = [grads[name][rows, block * D : (block + 1) * D] for name, block in members]
            if len(pieces) < 5:
                pieces.append(zero(48))
            if tile == len(tiles) - 1:
                pieces.append(jnp.concatenate([bias_ref[devs, :], zero(16, D - 128)], axis=1))
            else:
                pieces.append(zero(16))
            put(G, u, group, tile, mm(perm[0], jnp.concatenate(pieces, axis=0)).astype(bf16))
        if u % 2 == 1:
            piece = grads["fc2"][pl.ds(pl.multiple_of(group * 192, 16), 192), :]
            value = jnp.concatenate([piece, zero(64)], axis=0)
            put(G, u, group, 1, mm(perm[1], value).astype(bf16))


def permutations():
    out = np.zeros((2, 256, 256), np.float32)
    for o in range(256):
        if o < 240:
            k, rest = divmod(o, 48)
            dev, r = divmod(rest, 3)
            out[0, o, dev * 16 + k * 3 + r] = 1
        else:
            out[0, o, (o - 240) * 16 + 15] = 1
        if o < 192:
            dev, r = divmod(o, 12)
            out[1, o, dev * 16 + r] = 1
        else:
            dev, r = divmod(o - 192, 4)
            out[1, o, dev * 16 + 12 + r] = 1
    return np.concatenate([out, out.transpose(0, 2, 1)])


SHARDS = tuple(WEIGHTS)


def pack_own(place, own, G, rows_ref, line_ref):
    at = 0
    for name in ("ada", "qkv", "proj", "fc1"):
        width = WEIGHTS[name][0][2]
        own[name] = own["packed"].at[:, :, at : at + width]
        at += width
    lines = []
    for members in BIASES:
        line = None
        for name, at, width in members:
            line_ref[...] = jnp.zeros((8, 128), f32)
            line_ref[0:LAYERS, 0:width] = own[name][...].astype(f32)
            piece = line_ref[...]
            if at:
                piece = pltpu.roll(piece, at, 1)
            line = piece if line is None else line + piece
        lines.append(line)
    for u in range(UNITS):
        l = u // 2
        rows_ref[...] = jnp.zeros((BLOCK, D), f32)
        if u % 2 == 0:
            for tile, members in enumerate(ATTENTION_TILES):
                for k, (name, block) in enumerate(members):
                    row = tile * 16 + k * 3
                    rows_ref[row : row + 3, :] = own[name][
                        l, :, block * D : (block + 1) * D
                    ].astype(f32)
            rows_ref[31:32, 0:128] = lines[0][l : l + 1, :]
        else:
            for k, (name, block) in enumerate(MLP_TILE):
                rows_ref[k * 3 : k * 3 + 3, :] = own[name][
                    l, :, block * D : (block + 1) * D
                ].astype(f32)
            rows_ref[16:28, :] = own["fc2"][l].astype(f32)
            rows_ref[15:16, 0:128] = lines[1][l : l + 1, :]
        for p in range(PARTS):
            ref = slab(G, place, u, p, place.core, 0, place.turn(p, 0, 0))
            ref[...] = rows_ref[:, p * 128 : p * 128 + 128].astype(bf16)


def step_kernel(*refs):
    lat, cond, cot, table, counts = refs[:5]
    own = dict(zip(("packed", "fc2", "b_ada", "b_qv", "b_proj", "b_fc1", "b_fc2"), refs[5:12]))
    perm, back = refs[12].at[0:2], refs[12].at[2:4]
    act, glat, gcond, shard = refs[13:17]
    at = 17
    G, pair_in, f0, f1, f2, bias_ref, rows_ref, line_ref = refs[at : at + 8]
    at += 8
    gather_sems, scatter_sems = refs[at : at + 4], refs[at + 4 : at + 8]
    at += 8
    W = dict(zip(WEIGHTS, refs[at : at + 10]))
    grads = dict(zip(GRADS, refs[at + 10 : at + 19]))
    grads["fc1"] = grads["ada"].at[:, 0:FF]
    S = dict(zip(SCRATCH, refs[at + 19 :]))
    S.update(lat=lat, cot=cot, act_out=act, glat_out=glat)

    place = Place()
    greet(place, lambda: pack_own(place, own, G, rows_ref, line_ref))
    gather = Gather(place, G, gather_sems)
    for p in range(PARTS):
        gather.first(EVERY, p, 0)

    S["cond"][...] = jnp.zeros((8, D), f32)
    S["cond"][0:SLOTS, :] = cond[...].astype(f32)
    c = S["cond"][...]
    S["silu"][...] = (c / (1.0 + jnp.exp(-c))).astype(bf16)
    S["live"][...] = jnp.zeros((8, D), f32)
    for slot in range(SLOTS):
        alive = jnp.zeros((), f32)
        for position in range(SLOTS):
            chosen = (table[0, position] == slot) & (position < counts[0])
            alive = alive + jnp.where(chosen, 1.0, 0.0)
        S["live"][slot : slot + 1, :] = jnp.full((1, D), alive, f32)

    norm_first(S)
    queues = []

    def tick():
        for queue in queues:
            if queue:
                queue.pop(0)()

    def drain():
        while any(queues):
            tick()

    for p in range(PARTS):
        gather.arrive(EVERY, p, 0)
        gather.first(0, p, 1)
    for p in range(PARTS):
        gather.arrive(0, p, 1)
        gather.first(0, p, 2)
        gather.pair(0, p, 0, True).start()
    for p in range(PARTS):
        gather.first(LATER, p, 1)
    gather.forward(0)
    gather.close(0)
    for p in range(PARTS):
        gather.arrive(LATER, p, 1)
    gather.last(1)
    gather.wait_pair(0)
    unpack_unit(0, G, perm, W, bias_ref)

    def advance(u):
        gather.forward(u)
        if u + 1 < UNITS:
            gather.last(u + 1)

    def nothing():
        pass

    advance(1)
    queues.append([lambda: gather.close(1), nothing, lambda: advance(2), nothing, lambda: gather.close(2)])
    forward_attention(0, W, S, tick)
    gather.wait_pair(1)
    unpack_unit(1, G, perm, W, bias_ref)
    queues.append([lambda: advance(3), nothing, lambda: gather.close(3)])
    forward_mlp(0, W, S, tick)
    drain()
    gather.wait_pair(2)
    unpack_unit(2, G, perm, W, bias_ref)
    forward_attention(1, W, S, tick)
    gather.wait_pair(3)
    unpack_unit(3, G, perm, W, bias_ref)
    forward_mlp(1, W, S, tick)
    gather.wait_sends()

    scatter = Scatter(place, G, pair_in, (f0, f1, f2), scatter_sems)
    for l in reversed(range(LAYERS)):
        backward_mlp(l, W, S, grads, tick)
        pack_unit(2 * l + 1, G, back, grads, bias_ref)
        scatter.start(2 * l + 1)
        tick()
        one, two, three, four = scatter.events(2 * l + 1, shard)
        queues.append([nothing, one, nothing, two, three, four])
        backward_middle(l, W, S, grads, tick)
        backward_end(l, W, S, grads, tick)
        pack_unit(2 * l, G, back, grads, bias_ref)
        scatter.start(2 * l)
        tick()
        queues.append(scatter.events(2 * l, shard))
        backward_silu(l, W, S)
    sig = 1.0 / (1.0 + jnp.exp(-c))
    gcond[...] = S["gsilu"][...] * (sig * (1.0 + c * (1.0 - sig)))
    drain()
    for u in range(UNITS):
        scatter.wait_sends(u)


def run_step(args, perm):
    vmem = pl.BlockSpec(memory_space=pltpu.VMEM)
    smem = pl.BlockSpec(memory_space=pltpu.SMEM)
    ring = (UNITS, PARTS, 3, 4)
    scratch = [
        pltpu.VMEM(WHOLE, bf16),
        pltpu.VMEM((UNITS, PARTS, SIDE, SIDE, SIDE, BLOCK, 128), bf16),
        pltpu.VMEM((UNITS, PARTS, 3, BLOCK, 128), bf16),
        pltpu.VMEM((UNITS, PARTS, 3, SIDE, BLOCK, 128), bf16),
        pltpu.VMEM((UNITS, PARTS, 3, SIDE, SIDE, BLOCK, 128), bf16),
        pltpu.VMEM((DEVS, 128), bf16),
        pltpu.VMEM((BLOCK, D), f32),
        pltpu.VMEM((8, 128), f32),
        pltpu.SemaphoreType.DMA(ring),
        pltpu.SemaphoreType.DMA(ring),
        pltpu.SemaphoreType.DMA((UNITS, PARTS, 4)),
        pltpu.SemaphoreType.DMA((UNITS, PARTS, 4)),
        pltpu.SemaphoreType.DMA(ring),
        pltpu.SemaphoreType.DMA(ring),
        pltpu.SemaphoreType.DMA((UNITS, PARTS)),
        pltpu.SemaphoreType.DMA((UNITS, PARTS)),
    ]
    for table in (WEIGHTS, GRADS, SCRATCH):
        scratch += [pltpu.VMEM(s, t) for s, t in table.values()]
    return pl.pallas_call(
        step_kernel,
        out_shape=[
            jax.ShapeDtypeStruct((ROWS, D), bf16),
            jax.ShapeDtypeStruct((ROWS, D), bf16),
            jax.ShapeDtypeStruct((8, D), f32),
            jax.ShapeDtypeStruct((UNITS, PARTS, BLOCK, 128), f32),
        ],
        in_specs=[vmem] * 3 + [smem] * 2 + [vmem] * 8,
        out_specs=[vmem] * 4,
        scratch_shapes=scratch,
        compiler_params=pltpu.CompilerParams(
            collective_id=0, has_side_effects=True, vmem_limit_bytes=VMEM_BYTES
        ),
    )(*args, perm)


def finish_kernel(act_in, glat_in, gcond_in, shard, act, glat, gcond, *outs):
    act[...] = act_in[...]
    glat[...] = glat_in[...]
    gcond[...] = gcond_in[0:SLOTS, :]
    out = dict(zip(SHARDS, outs))
    for u in range(UNITS):
        l = u // 2
        tiles = ATTENTION_TILES if u % 2 == 0 else (MLP_TILE,)
        for p in range(PARTS):
            for tile, members in enumerate(tiles):
                for k, (name, block) in enumerate(members):
                    row = tile * 16 + k * 3
                    lanes = slice(block * D + p * 128, block * D + p * 128 + 128)
                    out[name][l, :, lanes] = shard[u, p, row : row + 3, :]
            if u % 2 == 1:
                out["fc2"][l, :, p * 128 : p * 128 + 128] = shard[u, p, 16:28, :]
        top = 24 if u % 2 == 0 else 8
        for name, at, width in BIASES[u % 2]:
            piece = shard[u, 0, top : top + 8, :]
            if at:
                piece = pltpu.roll(piece, 128 - at, 1)
            out[name][l : l + 1, :] = piece[7:8, 0:width]


def finish(act, glat, gcond, shard, shapes):
    vmem = pl.BlockSpec(memory_space=pltpu.VMEM)
    outs = [act, glat, jax.ShapeDtypeStruct((SLOTS, D), f32)]
    outs = [jax.ShapeDtypeStruct(o.shape, o.dtype) for o in outs]
    outs += [jax.ShapeDtypeStruct(s, f32) for s in shapes]
    return pl.pallas_call(
        finish_kernel,
        out_shape=outs,
        in_specs=[vmem] * 4,
        out_specs=[vmem] * len(outs),
    )(act, glat, gcond, shard)


def body(latents, condition, cotangent, slot_table, counts, *weights):
    perm = jnp.asarray(permutations(), bf16)
    args = (latents.reshape(ROWS, D), condition, cotangent.reshape(ROWS, D), slot_table, counts)
    own = dict(zip(SHARDS, weights))
    packed = jnp.concatenate([own[name] for name in ("ada", "qkv", "proj", "fc1")], axis=2)
    biases = tuple(own[name] for name in ("b_ada", "b_qv", "b_proj", "b_fc1", "b_fc2"))
    result = run_step(args + (packed, own["fc2"]) + biases, perm)
    act, glat, *rest = finish(*result, [w.shape for w in weights])
    return (act.reshape(SLOTS, LEN, D), glat.reshape(SLOTS, LEN, D), *rest)


def solution(mesh):
    split0 = (P("dp", None, None), P("dp", None), P("dp", None, None), P("dp", None), P("dp"))
    params = (P(None, "dp", None), P(None, "dp")) * 5
    outs = (P("dp", None, None), P("dp", None, None), P("dp", None)) + params
    return jax.shard_map(body, mesh=mesh, in_specs=split0 + params, out_specs=outs, check_vma=False)
```

```python
import functools
import jax
import jax.numpy as jnp
from jax import lax
from jax.experimental import pallas as pl
from jax.experimental.pallas import tpu as pltpu
from jax.sharding import PartitionSpec as P
import numpy as np

f32 = jnp.float32
bf16 = jnp.bfloat16
D = 384
HEADS = 6
FF = 1536
LAYERS = 2
LEN = 256
SLOTS = 2
ROWS = SLOTS * LEN
CHUNK = 64
STEPS = ROWS // CHUNK
EPS = 1e-06
GELU = 0.7978845608028654
VMEM_BYTES = 65280 * 1024


def mm(a, b):
    return lax.dot_general(a, b, (((1,), (0,)), ((), ())), preferred_element_type=f32)


def mm_t(a, b):
    return lax.dot_general(a, b, (((1,), (1,)), ((), ())), preferred_element_type=f32)


def t_mm(a, b):
    return lax.dot_general(a, b, (((0,), (0,)), ((), ())), preferred_element_type=f32)


def row_chunks(step):
    @pl.loop(0, STEPS, unroll=2)
    def _(i):
        rows = pl.ds(pl.multiple_of(i * CHUNK, CHUNK), CHUNK)
        slot = i // (STEPS // SLOTS)
        step(rows, slot)


def norm_parts(x):
    mean = jnp.mean(x, axis=-1, keepdims=True)
    centred = x - mean
    var = jnp.mean(centred * centred, axis=-1, keepdims=True)
    inv = lax.rsqrt(var + EPS)
    return centred * inv, inv


def norm_pull(u, n, inv):
    mean_u = jnp.mean(u, axis=-1, keepdims=True)
    mean_un = jnp.mean(u * n, axis=-1, keepdims=True)
    return inv * (u - mean_u - n * mean_un)


def keep_half(x, odd):
    lane = lax.broadcasted_iota(jnp.int32, (1, x.shape[1]), 1)
    mask = (lane >= 64) if odd else (lane < 64)
    return jnp.where(mask, x, jnp.zeros_like(x))


def keep_inv(S, rows, k, inv):
    lane = lax.broadcasted_iota(jnp.int32, (CHUNK, 128), 1)
    S["inv"][rows, :] = jnp.where(lane == k, inv, S["inv"][rows, :])


def mod_part(S, l, slot, k):
    return S["mod"][l, pl.ds(slot, 1), k * D : (k + 1) * D]


def norm_stream(l, S, rows):
    x = (S["lat"] if l == 0 else S["h"])[rows, :].astype(f32)
    n, inv = norm_parts(x)
    S["n_a"][l, rows, :] = n.astype(bf16)
    keep_inv(S, rows, l, inv)
    return n


def norm_first(S):
    def step(rows, slot):
        S["gn"][rows, :] = norm_stream(0, S, rows)

    row_chunks(step)


def forward_attention(l, W, S, tick):
    S["mod"][l] = mm(S["silu"][...], W["ada"][l]) + W["b_ada"][l]

    def prep(rows, slot):
        n = S["gn"][rows, :] if l == 0 else norm_stream(l, S, rows)
        S["normed"][l, rows, :] = (
            n * (1.0 + mod_part(S, l, slot, 1)) + mod_part(S, l, slot, 0)
        ).astype(bf16)

    row_chunks(prep)
    tick()
    for k in range(3):
        cols = slice(k * D, (k + 1) * D)
        out = mm(S["normed"][l], W["qkv"][l, :, cols])
        if k != 1:
            b = W["b_qv"][l, :, 0:D] if k == 0 else W["b_qv"][l, :, D:]
            out = out + b
        S["proj"][l, :, cols] = out.astype(bf16)
    tick()
    for slot in range(SLOTS):
        rows = slice(slot * LEN, slot * LEN + LEN)
        for pair in range(3):
            lanes = slice(pair * 128, pair * 128 + 128)
            q = (S["proj"][l, rows, lanes].astype(f32) * 0.125).astype(bf16)
            k = S["proj"][l, rows, D + pair * 128 : D + pair * 128 + 128]
            v = S["proj"][l, rows, 2 * D + pair * 128 : 2 * D + pair * 128 + 128]
            att = None
            for odd in range(2):
                s = mm_t(keep_half(q, odd), k)
                e = jnp.exp(s - jnp.max(s, axis=-1, keepdims=True))
                p = (e * (1.0 / jnp.sum(e, axis=-1, keepdims=True))).astype(bf16)
                S["prob"][l, slot * HEADS + pair * 2 + odd] = p
                term = mm(p, keep_half(v, odd))
                att = term if att is None else att + term
            S["att"][l, rows, lanes] = att.astype(bf16)
        tick()
    S["gn"][...] = mm(S["att"][l], W["proj"][l]) + W["b_proj"][l]
    tick()


def forward_mlp(l, W, S, tick):
    def middle(rows, slot):
        x = (S["lat"] if l == 0 else S["h"])[rows, :].astype(f32)
        branch = S["gn"][rows, :]
        S["branch"][l, rows, :] = branch.astype(bf16)
        m = x + mod_part(S, l, slot, 2) * branch
        S["h"][rows, :] = m
        n, inv = norm_parts(m)
        S["n_m"][l, rows, :] = n.astype(bf16)
        keep_inv(S, rows, LAYERS + l, inv)
        S["normed_m"][l, rows, :] = (
            n * (1.0 + mod_part(S, l, slot, 4)) + mod_part(S, l, slot, 3)
        ).astype(bf16)

    row_chunks(middle)
    tick()
    for part in range(2):

        @pl.loop(0, FF // 512, unroll=True)
        def _(j):
            cols = pl.ds(pl.multiple_of(part * (FF // 2) + j * 256, 256), 256)
            x = mm(S["normed_m"][l], W["fc1"][l, :, cols]) + W["b_fc1"][l, :, cols]
            x2 = x * x
            t = jnp.tanh(GELU * (x + 0.044715 * (x2 * x)))
            half = 0.5 * (1.0 + t)
            S["activated"][l, :, cols] = (x * half).astype(bf16)
            slope = half + 0.5 * x * (1.0 - t * t) * (GELU * (1.0 + 3 * 0.044715 * x2))
            S["slope"][l, :, cols] = slope.astype(bf16)

        tick()
    S["gn"][...] = mm(S["activated"][l], W["fc2"][l]) + W["b_fc2"][l]

    def finish(rows, slot):
        output = S["gn"][rows, :]
        S["output"][l, rows, :] = output.astype(bf16)
        r = S["h"][rows, :] + mod_part(S, l, slot, 5) * output
        if l == LAYERS - 1:
            S["act_out"][rows, :] = (r * S["live"][pl.ds(slot, 1), :]).astype(bf16)
        else:
            S["h"][rows, :] = r

    row_chunks(finish)
    tick()


def add_mod(S, l, slot, k, value):
    cols = slice(k * D, (k + 1) * D)
    S["gmod"][l, pl.ds(slot, 1), cols] += jnp.sum(value, axis=0, keepdims=True)


def backward_mlp(l, W, S, G, tick):
    ones = jnp.ones((8, ROWS), bf16)
    S["gmod"][l] = jnp.zeros((8, 6 * D), f32)

    def start(rows, slot):
        if l == LAYERS - 1:
            g = S["cot"][rows, :].astype(f32) * S["live"][pl.ds(slot, 1), :]
            S["h"][rows, :] = g
        else:
            g = S["h"][rows, :]
        add_mod(S, l, slot, 5, g * S["output"][l, rows, :].astype(f32))
        S["go"][rows, :] = (mod_part(S, l, slot, 5) * g).astype(bf16)

    row_chunks(start)
    go = S["go"]
    G["b_fc2"][...] = mm(ones, go[...])[0:1]
    for part in range(2):

        @pl.loop(0, FF // 512, unroll=True)
        def _(j):
            cols = pl.ds(pl.multiple_of(part * (FF // 2) + j * 256, 256), 256)
            gh = mm_t(go[...], W["fc2"][l, cols, :]) * S["slope"][l, :, cols].astype(f32)
            gh = gh.astype(bf16)
            G["fc2"][cols, :] = t_mm(S["activated"][l, :, cols], go[...]).astype(bf16)
            S["activated"][l, :, cols] = gh
            G["fc1"][:, cols] = t_mm(S["normed_m"][l], gh).astype(bf16)
            G["b_fc1"][:, cols] = mm(ones, gh)[0:1]

    tick()


def backward_middle(l, W, S, G, tick):
    ones = jnp.ones((8, ROWS), bf16)
    go = S["go"]
    S["gn"][...] = mm_t(S["activated"][l], W["fc1"][l])

    def mid(rows, slot):
        gn = S["gn"][rows, :]
        n = S["n_m"][l, rows, :].astype(f32)
        inv = S["inv"][rows, LAYERS + l : LAYERS + l + 1]
        add_mod(S, l, slot, 3, gn)
        add_mod(S, l, slot, 4, gn * n)
        gm = S["h"][rows, :] + norm_pull((1.0 + mod_part(S, l, slot, 4)) * gn, n, inv)
        S["h"][rows, :] = gm
        add_mod(S, l, slot, 2, gm * S["branch"][l, rows, :].astype(f32))
        S["go"][rows, :] = (mod_part(S, l, slot, 2) * gm).astype(bf16)

    row_chunks(mid)
    G["b_proj"][...] = mm(ones, go[...])[0:1]
    G["proj"][...] = t_mm(S["att"][l], go[...]).astype(bf16)
    S["att"][l] = mm_t(go[...], W["proj"][l]).astype(bf16)
    tick()
    for slot in range(SLOTS):
        rows = slice(slot * LEN, slot * LEN + LEN)
        for pair in range(3):
            lanes = slice(pair * 128, pair * 128 + 128)
            kl = slice(D + pair * 128, D + pair * 128 + 128)
            vl = slice(2 * D + pair * 128, 2 * D + pair * 128 + 128)
            q = S["proj"][l, rows, lanes]
            k = S["proj"][l, rows, kl]
            v = S["proj"][l, rows, vl]
            ga = S["att"][l, rows, lanes]
            gq = gk = gv = None
            for odd in range(2):
                low = S["prob"][l, slot * HEADS + pair * 2 + odd]
                p = low.astype(f32)
                ga_h = keep_half(ga, odd)
                gp = mm_t(ga_h, v)
                dot = jnp.sum(p * gp, axis=-1, keepdims=True)
                gs = (p * (gp - dot)).astype(bf16)
                tv = t_mm(low, ga_h)
                tq = mm(gs, keep_half(k, odd))
                tk = t_mm(gs, keep_half(q, odd))
                gv = tv if gv is None else gv + tv
                gq = tq if gq is None else gq + tq
                gk = tk if gk is None else gk + tk
            S["proj"][l, rows, lanes] = (gq * 0.125).astype(bf16)
            S["proj"][l, rows, kl] = (gk * 0.125).astype(bf16)
            S["proj"][l, rows, vl] = gv.astype(bf16)
        tick()


def backward_end(l, W, S, G, tick):
    ones = jnp.ones((8, ROWS), bf16)
    for k in range(3):
        cols = slice(k * D, (k + 1) * D)
        gpk = S["proj"][l, :, cols]
        G["qkv"][:, cols] = t_mm(S["normed"][l], gpk).astype(bf16)
        if k != 1:
            G["b_qv"][:, (k // 2) * D : (k // 2 + 1) * D] = mm(ones, gpk)[0:1]
    S["gn"][...] = mm_t(S["proj"][l], W["qkv"][l])
    tick()

    def last(rows, slot):
        gn = S["gn"][rows, :]
        n = S["n_a"][l, rows, :].astype(f32)
        inv = S["inv"][rows, l : l + 1]
        add_mod(S, l, slot, 0, gn)
        add_mod(S, l, slot, 1, gn * n)
        g = S["h"][rows, :] + norm_pull((1.0 + mod_part(S, l, slot, 1)) * gn, n, inv)
        if l == 0:
            S["glat_out"][rows, :] = g.astype(bf16)
        else:
            S["h"][rows, :] = g

    row_chunks(last)
    gm = S["gmod"][l]
    hi = gm.astype(bf16)
    lo = (gm - hi.astype(f32)).astype(bf16)
    silu = S["silu"][...]
    eight = jnp.ones((8, 8), bf16)
    G["b_ada"][...] = (mm(eight, hi) + mm(eight, lo))[0:1]
    G["ada"][...] = (t_mm(silu, hi) + t_mm(silu, lo)).astype(bf16)


def backward_silu(l, W, S):
    gm = S["gmod"][l]
    hi = gm.astype(bf16)
    lo = (gm - hi.astype(f32)).astype(bf16)
    w = W["ada"][l]
    grad_silu = mm_t(hi, w) + mm_t(lo, w)
    if l == LAYERS - 1:
        S["gsilu"][...] = grad_silu
    else:
        S["gsilu"][...] += grad_silu


SCRATCH = dict(
    cond=((8, D), f32),
    live=((8, D), f32),
    mod=((LAYERS, 8, 6 * D), f32),
    gmod=((LAYERS, 8, 6 * D), f32),
    silu=((8, D), bf16),
    gsilu=((8, D), f32),
    h=((ROWS, D), f32),
    go=((ROWS, D), bf16),
    gn=((ROWS, D), f32),
    n_a=((LAYERS, ROWS, D), bf16),
    n_m=((LAYERS, ROWS, D), bf16),
    inv=((ROWS, 128), f32),
    normed=((LAYERS, ROWS, D), bf16),
    normed_m=((LAYERS, ROWS, D), bf16),
    proj=((LAYERS, ROWS, 3 * D), bf16),
    prob=((LAYERS, SLOTS * HEADS, LEN, LEN), bf16),
    att=((LAYERS, ROWS, D), bf16),
    branch=((LAYERS, ROWS, D), bf16),
    activated=((LAYERS, ROWS, FF), bf16),
    slope=((LAYERS, ROWS, FF), bf16),
    output=((LAYERS, ROWS, D), bf16),
)
WEIGHTS = dict(
    ada=((LAYERS, D, 6 * D), bf16),
    b_ada=((LAYERS, 1, 6 * D), f32),
    qkv=((LAYERS, D, 3 * D), bf16),
    b_qv=((LAYERS, 1, 2 * D), f32),
    proj=((LAYERS, D, D), bf16),
    b_proj=((LAYERS, 1, D), f32),
    fc1=((LAYERS, D, FF), bf16),
    b_fc1=((LAYERS, 1, FF), f32),
    fc2=((LAYERS, FF, D), bf16),
    b_fc2=((LAYERS, 1, D), f32),
)
GRADS = dict(
    ada=((D, 6 * D), bf16),
    b_ada=((1, 6 * D), f32),
    qkv=((D, 3 * D), bf16),
    b_qv=((1, 2 * D), f32),
    proj=((D, D), bf16),
    b_proj=((1, D), f32),
    b_fc1=((1, FF), f32),
    fc2=((FF, D), bf16),
    b_fc2=((1, D), f32),
)

MESH = pl.DeviceIdType.MESH
STRIDE = (2, 8, 32)
ORDER = ((0, 1, 2), (1, 2, 0), (2, 0, 1))
PARTS = 3
SIDE = 4
DEVS = 128
UNITS = 4
BLOCK = 32
HALF = BLOCK // 2
GROUPS = DEVS // 16
WHOLE = (UNITS, PARTS, 2, SIDE, SIDE, SIDE, BLOCK, 128)


class Place:
    def __init__(self):
        me = lax.axis_index("dp")
        self.core = me % 2
        self.at = ((me // 2) % 4, (me // 8) % 4, me // 32)
        self.me = me
        self.sibling = me + 1 - 2 * self.core

    def beside(self, axis, step):
        here = self.at[axis]
        return self.me + ((here + step) % 4 - here) * STRIDE[axis]

    def turn(self, p, phase, step):
        return (self.at[ORDER[p][phase]] + step) % 4


def greet(place, between):
    barrier = pltpu.get_barrier_semaphore()
    for axis in range(3):
        for step in (1, 2, 3):
            pl.semaphore_signal(
                barrier, inc=1, device_id=(place.beside(axis, step),), device_id_type=MESH
            )
    pl.semaphore_signal(barrier, inc=1, device_id=(place.sibling,), device_id_type=MESH)
    between()
    pl.semaphore_wait(barrier, 10)


def slab(G, place, u, p, core, phase, j, half=None):
    i2 = place.at[ORDER[p][2]]
    i1 = place.at[ORDER[p][1]]
    rows = slice(None) if half is None else slice(half * HALF, half * HALF + HALF)
    if phase == 0:
        return G.at[u, p, core, i2, i1, j, rows, :]
    if phase == 1:
        return G.at[u, p, core, i2, j, :, rows, :]
    return G.at[u, p, core, j, :, :, rows, :]


def remote(src, dst, send, recv, target):
    return pltpu.make_async_remote_copy(
        src_ref=src,
        dst_ref=dst,
        send_sem=send,
        recv_sem=recv,
        device_id=(target,),
        device_id_type=MESH,
    )


DIRECT = (2, 1, 3)
EVERY = slice(0, UNITS)
LATER = slice(1, UNITS)
RING_OUT = ((0, None, 1), (0, None, 3), (3, 0, 1), (1, 1, 3))
RING_IN = ((3, None, 3), (1, None, 1), (2, 0, 3), (2, 1, 1))


class Gather:
    def __init__(self, place, G, sems):
        self.place, self.G = place, G
        self.send, self.recv, self.send_pair, self.recv_pair = sems

    def copy(self, u, p, phase, kind, arriving=False):
        place = self.place
        s = u.start if isinstance(u, slice) else u
        axis = ORDER[p][phase]
        half = None
        if phase < 2:
            step = DIRECT[kind]
            other = 4 - step if arriving else step
            j = 4 - step if arriving else 0
        else:
            j, half, other = (RING_IN if arriving else RING_OUT)[kind]
        ref = slab(self.G, place, u, p, place.core, phase, place.turn(p, phase, j), half)
        return remote(
            ref,
            ref,
            self.send.at[s, p, phase, kind],
            self.recv.at[s, p, phase, kind],
            place.beside(axis, other),
        )

    def pair(self, u, p, kind, mine):
        place = self.place
        step = (0, 3, 1, 2)[kind]
        core = place.core if mine else 1 - place.core
        ref = slab(self.G, place, u, p, core, 2, place.turn(p, 2, step))
        return remote(
            ref, ref, self.send_pair.at[u, p, kind], self.recv_pair.at[u, p, kind], place.sibling
        )

    def first(self, u, p, phase):
        for kind in range(3 if phase < 2 else 2):
            self.copy(u, p, phase, kind).start()

    def arrive(self, u, p, phase):
        for kind in (1, 2, 0):
            self.copy(u, p, phase, kind, True).wait_recv()

    def last(self, u):
        for p in range(PARTS):
            self.first(u, p, 2)
            self.pair(u, p, 0, True).start()

    def forward(self, u):
        for p in range(PARTS):
            for kind in (0, 1):
                self.copy(u, p, 2, kind, True).wait_recv()
                self.copy(u, p, 2, 2 + kind).start()
                self.pair(u, p, 1 + kind, True).start()

    def close(self, u):
        for p in range(PARTS):
            for kind in (2, 3):
                self.copy(u, p, 2, kind, True).wait_recv()
            self.pair(u, p, 3, True).start()

    def wait_pair(self, u):
        for p in range(PARTS):
            for kind in range(4):
                self.pair(u, p, kind, False).wait_recv()

    def wait_sends(self):
        for p in range(PARTS):
            for kind in range(3):
                self.copy(EVERY, p, 0, kind).wait_send()
                self.copy(0, p, 1, kind).wait_send()
                self.copy(LATER, p, 1, kind).wait_send()
            for u in range(UNITS):
                for kind in range(4):
                    self.copy(u, p, 2, kind).wait_send()
                    self.pair(u, p, kind, True).wait_send()


class Scatter:
    def __init__(self, place, G, pair_in, full_in, sems):
        self.place, self.G = place, G
        self.pair_in, self.full_in = pair_in, full_in
        self.send, self.recv, self.send_pair, self.recv_pair = sems

    def pair(self, u, p, half):
        place = self.place
        blocks = [slice(None)] * 3
        blocks[2 - ORDER[p].index(2)] = slice(half * 2, half * 2 + 2)
        return remote(
            self.G.at[(u, p, 1 - place.core, *blocks)],
            self.pair_in.at[(u, p, *blocks)],
            self.send_pair.at[u, p, half],
            self.recv_pair.at[u, p, half],
            place.sibling,
        )

    def start(self, u, half):
        for p in range(PARTS):
            self.pair(u, p, half).start()

    def copy(self, u, p, phase, kind):
        place = self.place
        step = DIRECT[kind]
        return remote(
            slab(self.G, place, u, p, place.core, phase, place.turn(p, phase, step)),
            self.full_in[phase].at[u, p, kind],
            self.send.at[u, p, phase, kind],
            self.recv.at[u, p, phase, kind],
            place.beside(ORDER[p][phase], step),
        )

    def first(self, u, p, phase):
        for kind in range(3):
            self.copy(u, p, phase, kind).start()

    def add_pair(self, u):
        place = self.place
        for p in range(PARTS):
            for half in range(2):
                self.pair(u, p, half).wait_recv()
            for kind in range(4):
                j = place.turn(p, 2, (DIRECT + (0,))[kind])
                target = self.G.at[u, p, place.core, j]
                source = self.pair_in.at[u, p, j]

                @pl.loop(0, SIDE)
                def _(k):
                    target[k] = (target[k].astype(f32) + source[k].astype(f32)).astype(bf16)

                if kind < 3:
                    self.copy(u, p, 2, kind).start()

    def direct(self, u, phase, out_ref):
        place = self.place
        for p in range(PARTS):
            for kind in (1, 2, 0):
                self.copy(u, p, phase, kind).wait_recv()
            target = slab(self.G, place, u, p, place.core, phase, place.turn(p, phase, 0))
            parts = [self.full_in[phase].at[u, p, kind] for kind in range(3)]

            def total(*at):
                a, b, c = (part[at].astype(f32) for part in parts)
                return (target[at].astype(f32) + a) + (b + c)

            if phase == 0:
                out_ref[u, p] = total(slice(None))
                continue
            if phase == 1:
                target[...] = total(slice(None)).astype(bf16)
            else:

                @pl.loop(0, SIDE)
                def _(k):
                    target[k] = total(k).astype(bf16)

            self.first(u, p, phase - 1)

    def events(self, u, out_ref):
        return [
            lambda: self.add_pair(u),
            lambda: self.direct(u, 2, out_ref),
            lambda: self.direct(u, 1, out_ref),
            lambda: self.direct(u, 0, out_ref),
        ]

    def wait_sends(self, u):
        for p in range(PARTS):
            for half in range(2):
                self.pair(u, p, half).wait_send()
            for phase in range(3):
                for kind in range(3):
                    self.copy(u, p, phase, kind).wait_send()


def tile_refs(G, u, group, tile):
    z = group // 2
    for p in range(PARTS):
        for i in range(16):
            y_low, x, core = i // 8, (i // 2) % 4, i % 2
            at = (x, (group % 2) * 2 + y_low, z)
            o = ORDER[p]
            yield p, i, G.at[
                u, p, core, at[o[2]], at[o[1]], at[o[0]], tile * 16 : tile * 16 + 16, :
            ]


def pick(G, u, group, tile):
    parts = [[], [], []]
    for p, i, ref in tile_refs(G, u, group, tile):
        parts[p].append(ref[...])
    return jnp.concatenate([jnp.concatenate(part, axis=0) for part in parts], axis=1)


def put(G, u, group, tile, value):
    for p, i, ref in tile_refs(G, u, group, tile):
        ref[...] = value[i * 16 : i * 16 + 16, p * 128 : p * 128 + 128]


ATTENTION_TILES = (
    tuple(("ada", k) for k in range(5)),
    (("ada", 5), ("qkv", 0), ("qkv", 1), ("qkv", 2), ("proj", 0)),
)
MLP_TILE = (("fc1", 0), ("fc1", 1), ("fc1", 2), ("fc1", 3))
BIASES = (
    (("b_ada", 0, 18), ("b_qv", 18, 6), ("b_proj", 24, 3)),
    (("b_fc1", 0, 12), ("b_fc2", 12, 3)),
)


LINE = 32


def spread(at, width, start):
    count = {18: 48, 12: 32, 6: 64, 3: 128}[width]
    top = min(start // width // 16 * 16, DEVS - count)
    n = lax.broadcasted_iota(jnp.int32, (1, D), 1).astype(f32) + float(start)
    owner = jnp.floor((n + 0.5) * (1.0 / width))
    lane = (n - width * owner) + float(at)
    row = lax.broadcasted_iota(jnp.int32, (count, D), 0).astype(f32)
    which = lax.broadcasted_iota(jnp.int32, (LINE, D), 0).astype(f32)
    return top, count, row == owner - float(top), jnp.where(which == lane, 1.0, 0.0).astype(bf16)


def unpack_bias(u, W, bias_ref):
    for name, at, width in BIASES[u % 2]:
        for start in range(0, DEVS * width, D):
            top, count, owner, lane = spread(at, width, start)
            value = mm(bias_ref[top : top + count, 0:LINE], lane)
            value = mm(jnp.ones((8, count), bf16), jnp.where(owner, value, 0.0).astype(bf16))
            W[name][u // 2, :, start : start + D] = value[0:1, :]


def pack_bias(u, grads, bias_ref):
    total = jnp.zeros((DEVS, DEVS), f32)
    for name, at, width in BIASES[u % 2]:
        for start in range(0, DEVS * width, D):
            top, count, owner, lane = spread(at, width, start)
            value = jnp.where(owner, grads[name][0:1, start : start + D], 0.0).astype(bf16)
            lane = jnp.concatenate([lane, jnp.zeros((DEVS - LINE, D), bf16)], axis=0)
            pieces = [mm_t(value, lane)]
            if top:
                pieces.insert(0, jnp.zeros((top, DEVS), f32))
            if top + count < DEVS:
                pieces.append(jnp.zeros((DEVS - top - count, DEVS), f32))
            total = total + (jnp.concatenate(pieces, axis=0) if len(pieces) > 1 else pieces[0])
    bias_ref[...] = total.astype(bf16)


def unpack_unit(u, G, perm, W, bias_ref):
    l = u // 2

    @pl.loop(0, GROUPS, unroll=4)
    def _(group):
        rows = pl.ds(pl.multiple_of(group * 48, 16), 48)
        devs = pl.ds(pl.multiple_of(group * 16, 16), 16)
        tiles = ATTENTION_TILES if u % 2 == 0 else (MLP_TILE,)
        for tile, members in enumerate(tiles):
            out = mm(perm[0], pick(G, u, group, tile)).astype(bf16)
            for k, (name, block) in enumerate(members):
                W[name][l, rows, block * D : (block + 1) * D] = out[k * 48 : k * 48 + 48, :]
            if tile == len(tiles) - 1:
                bias_ref[devs, :] = out[240:256, 0:128]
        if u % 2 == 1:
            out = mm(perm[1], pick(G, u, group, 1)).astype(bf16)
            W["fc2"][l, pl.ds(pl.multiple_of(group * 192, 16), 192), :] = out[0:192, :]

    unpack_bias(u, W, bias_ref)


def pack_unit(u, G, perm, grads, bias_ref, started):
    pack_bias(u, grads, bias_ref)

    def zero(n, width=D):
        return jnp.zeros((n, width), bf16)

    def pack_group(group):
        rows = pl.ds(pl.multiple_of(group * 48, 16), 48)
        devs = pl.ds(pl.multiple_of(group * 16, 16), 16)
        tiles = ATTENTION_TILES if u % 2 == 0 else (MLP_TILE,)
        for tile, members in enumerate(tiles):
            pieces = [grads[name][rows, block * D : (block + 1) * D] for name, block in members]
            if len(pieces) < 5:
                pieces.append(zero(48))
            if tile == len(tiles) - 1:
                pieces.append(jnp.concatenate([bias_ref[devs, :], zero(16, D - 128)], axis=1))
            else:
                pieces.append(zero(16))
            put(G, u, group, tile, mm(perm[0], jnp.concatenate(pieces, axis=0)).astype(bf16))
        if u % 2 == 1:
            piece = grads["fc2"][pl.ds(pl.multiple_of(group * 192, 16), 192), :]
            value = jnp.concatenate([piece, zero(64)], axis=0)
            put(G, u, group, 1, mm(perm[1], value).astype(bf16))

    for half in range(2):
        pl.loop(half * GROUPS // 2, (half + 1) * GROUPS // 2, unroll=4)(pack_group)
        started(u, half)


def permutations():
    out = np.zeros((2, 256, 256), np.float32)
    for o in range(256):
        if o < 240:
            k, rest = divmod(o, 48)
            dev, r = divmod(rest, 3)
            out[0, o, dev * 16 + k * 3 + r] = 1
        else:
            out[0, o, (o - 240) * 16 + 15] = 1
        if o < 192:
            dev, r = divmod(o, 12)
            out[1, o, dev * 16 + r] = 1
        else:
            dev, r = divmod(o - 192, 4)
            out[1, o, dev * 16 + 12 + r] = 1
    return np.concatenate([out, out.transpose(0, 2, 1)])


SHARDS = tuple(WEIGHTS)


def pack_own(place, own, G, rows_ref, line_ref):
    at = 0
    for name in ("ada", "qkv", "proj", "fc1"):
        width = WEIGHTS[name][0][2]
        own[name] = own["packed"].at[:, :, at : at + width]
        at += width
    lines = []
    for members in BIASES:
        line = None
        for name, at, width in members:
            line_ref[...] = jnp.zeros((8, 128), f32)
            line_ref[0:LAYERS, 0:width] = own[name][...].astype(f32)
            piece = line_ref[...]
            if at:
                piece = pltpu.roll(piece, at, 1)
            line = piece if line is None else line + piece
        lines.append(line)
    for u in range(UNITS):
        l = u // 2
        rows_ref[...] = jnp.zeros((BLOCK, D), f32)
        if u % 2 == 0:
            for tile, members in enumerate(ATTENTION_TILES):
                for k, (name, block) in enumerate(members):
                    row = tile * 16 + k * 3
                    rows_ref[row : row + 3, :] = own[name][
                        l, :, block * D : (block + 1) * D
                    ].astype(f32)
            rows_ref[31:32, 0:128] = lines[0][l : l + 1, :]
        else:
            for k, (name, block) in enumerate(MLP_TILE):
                rows_ref[k * 3 : k * 3 + 3, :] = own[name][
                    l, :, block * D : (block + 1) * D
                ].astype(f32)
            rows_ref[16:28, :] = own["fc2"][l].astype(f32)
            rows_ref[15:16, 0:128] = lines[1][l : l + 1, :]
        for p in range(PARTS):
            ref = slab(G, place, u, p, place.core, 0, place.turn(p, 0, 0))
            ref[...] = rows_ref[:, p * 128 : p * 128 + 128].astype(bf16)


def step_kernel(*refs):
    lat, cond, cot, table, counts = refs[:5]
    own = dict(zip(("packed", "fc2", "b_ada", "b_qv", "b_proj", "b_fc1", "b_fc2"), refs[5:12]))
    perm, back = refs[12].at[0:2], refs[12].at[2:4]
    act, glat, gcond, shard = refs[13:17]
    at = 17
    G, pair_in, f0, f1, f2, bias_ref, rows_ref, line_ref = refs[at : at + 8]
    at += 8
    gather_sems, scatter_sems = refs[at : at + 4], refs[at + 4 : at + 8]
    at += 8
    W = dict(zip(WEIGHTS, refs[at : at + 10]))
    grads = dict(zip(GRADS, refs[at + 10 : at + 19]))
    grads["fc1"] = grads["ada"].at[:, 0:FF]
    S = dict(zip(SCRATCH, refs[at + 19 :]))
    S.update(lat=lat, cot=cot, act_out=act, glat_out=glat)

    place = Place()
    greet(place, lambda: pack_own(place, own, G, rows_ref, line_ref))
    gather = Gather(place, G, gather_sems)
    for p in range(PARTS):
        gather.first(EVERY, p, 0)

    S["cond"][...] = jnp.zeros((8, D), f32)
    S["cond"][0:SLOTS, :] = cond[...].astype(f32)
    c = S["cond"][...]
    S["silu"][...] = (c / (1.0 + jnp.exp(-c))).astype(bf16)
    S["live"][...] = jnp.zeros((8, D), f32)
    for slot in range(SLOTS):
        alive = jnp.zeros((), f32)
        for position in range(SLOTS):
            chosen = (table[0, position] == slot) & (position < counts[0])
            alive = alive + jnp.where(chosen, 1.0, 0.0)
        S["live"][slot : slot + 1, :] = jnp.full((1, D), alive, f32)

    norm_first(S)
    queues = []

    def tick():
        for queue in queues:
            if queue:
                queue.pop(0)()

    def drain():
        while any(queues):
            tick()

    for p in range(PARTS):
        gather.arrive(EVERY, p, 0)
        gather.first(0, p, 1)
    for p in range(PARTS):
        gather.arrive(0, p, 1)
        gather.first(0, p, 2)
        gather.pair(0, p, 0, True).start()
    for p in range(PARTS):
        gather.first(LATER, p, 1)
    gather.forward(0)
    gather.close(0)
    for p in range(PARTS):
        gather.arrive(LATER, p, 1)
    gather.last(1)
    gather.wait_pair(0)
    unpack_unit(0, G, perm, W, bias_ref)

    def advance(u):
        gather.forward(u)
        if u + 1 < UNITS:
            gather.last(u + 1)

    def nothing():
        pass

    advance(1)
    queues.append([lambda: gather.close(1), nothing, lambda: advance(2), nothing, lambda: gather.close(2)])
    forward_attention(0, W, S, tick)
    gather.wait_pair(1)
    unpack_unit(1, G, perm, W, bias_ref)
    queues.append([lambda: advance(3), nothing, lambda: gather.close(3)])
    forward_mlp(0, W, S, tick)
    drain()
    gather.wait_pair(2)
    unpack_unit(2, G, perm, W, bias_ref)
    forward_attention(1, W, S, tick)
    gather.wait_pair(3)
    unpack_unit(3, G, perm, W, bias_ref)
    forward_mlp(1, W, S, tick)
    gather.wait_sends()

    scatter = Scatter(place, G, pair_in, (f0, f1, f2), scatter_sems)
    for l in reversed(range(LAYERS)):
        backward_mlp(l, W, S, grads, tick)
        pack_unit(2 * l + 1, G, back, grads, bias_ref, scatter.start)
        tick()
        one, two, three, four = scatter.events(2 * l + 1, shard)
        queues.append([nothing, one, nothing, two, three, four])
        backward_middle(l, W, S, grads, tick)
        backward_end(l, W, S, grads, tick)
        pack_unit(2 * l, G, back, grads, bias_ref, scatter.start)
        tick()
        queues.append(scatter.events(2 * l, shard))
        backward_silu(l, W, S)
    sig = 1.0 / (1.0 + jnp.exp(-c))
    gcond[...] = S["gsilu"][...] * (sig * (1.0 + c * (1.0 - sig)))
    drain()
    for u in range(UNITS):
        scatter.wait_sends(u)


def run_step(args, perm):
    vmem = pl.BlockSpec(memory_space=pltpu.VMEM)
    smem = pl.BlockSpec(memory_space=pltpu.SMEM)
    ring = (UNITS, PARTS, 3, 4)
    scratch = [
        pltpu.VMEM(WHOLE, bf16),
        pltpu.VMEM((UNITS, PARTS, SIDE, SIDE, SIDE, BLOCK, 128), bf16),
        pltpu.VMEM((UNITS, PARTS, 3, BLOCK, 128), bf16),
        pltpu.VMEM((UNITS, PARTS, 3, SIDE, BLOCK, 128), bf16),
        pltpu.VMEM((UNITS, PARTS, 3, SIDE, SIDE, BLOCK, 128), bf16),
        pltpu.VMEM((DEVS, 128), bf16),
        pltpu.VMEM((BLOCK, D), f32),
        pltpu.VMEM((8, 128), f32),
        pltpu.SemaphoreType.DMA(ring),
        pltpu.SemaphoreType.DMA(ring),
        pltpu.SemaphoreType.DMA((UNITS, PARTS, 4)),
        pltpu.SemaphoreType.DMA((UNITS, PARTS, 4)),
        pltpu.SemaphoreType.DMA(ring),
        pltpu.SemaphoreType.DMA(ring),
        pltpu.SemaphoreType.DMA((UNITS, PARTS, 2)),
        pltpu.SemaphoreType.DMA((UNITS, PARTS, 2)),
    ]
    for table in (WEIGHTS, GRADS, SCRATCH):
        scratch += [pltpu.VMEM(s, t) for s, t in table.values()]
    return pl.pallas_call(
        step_kernel,
        out_shape=[
            jax.ShapeDtypeStruct((ROWS, D), bf16),
            jax.ShapeDtypeStruct((ROWS, D), bf16),
            jax.ShapeDtypeStruct((8, D), f32),
            jax.ShapeDtypeStruct((UNITS, PARTS, BLOCK, 128), f32),
        ],
        in_specs=[vmem] * 3 + [smem] * 2 + [vmem] * 8,
        out_specs=[vmem] * 4,
        scratch_shapes=scratch,
        compiler_params=pltpu.CompilerParams(
            collective_id=0, has_side_effects=True, vmem_limit_bytes=VMEM_BYTES
        ),
    )(*args, perm)


def finish_kernel(act_in, glat_in, gcond_in, shard, act, glat, gcond, *outs):
    act[...] = act_in[...]
    glat[...] = glat_in[...]
    gcond[...] = gcond_in[0:SLOTS, :]
    out = dict(zip(SHARDS, outs))
    for u in range(UNITS):
        l = u // 2
        tiles = ATTENTION_TILES if u % 2 == 0 else (MLP_TILE,)
        for p in range(PARTS):
            for tile, members in enumerate(tiles):
                for k, (name, block) in enumerate(members):
                    row = tile * 16 + k * 3
                    lanes = slice(block * D + p * 128, block * D + p * 128 + 128)
                    out[name][l, :, lanes] = shard[u, p, row : row + 3, :]
            if u % 2 == 1:
                out["fc2"][l, :, p * 128 : p * 128 + 128] = shard[u, p, 16:28, :]
        top = 24 if u % 2 == 0 else 8
        for name, at, width in BIASES[u % 2]:
            piece = shard[u, 0, top : top + 8, :]
            if at:
                piece = pltpu.roll(piece, 128 - at, 1)
            out[name][l : l + 1, :] = piece[7:8, 0:width]


def finish(act, glat, gcond, shard, shapes):
    vmem = pl.BlockSpec(memory_space=pltpu.VMEM)
    outs = [act, glat, jax.ShapeDtypeStruct((SLOTS, D), f32)]
    outs = [jax.ShapeDtypeStruct(o.shape, o.dtype) for o in outs]
    outs += [jax.ShapeDtypeStruct(s, f32) for s in shapes]
    return pl.pallas_call(
        finish_kernel,
        out_shape=outs,
        in_specs=[vmem] * 4,
        out_specs=[vmem] * len(outs),
    )(act, glat, gcond, shard)


def body(latents, condition, cotangent, slot_table, counts, *weights):
    perm = jnp.asarray(permutations(), bf16)
    args = (latents.reshape(ROWS, D), condition, cotangent.reshape(ROWS, D), slot_table, counts)
    own = dict(zip(SHARDS, weights))
    packed = jnp.concatenate([own[name] for name in ("ada", "qkv", "proj", "fc1")], axis=2)
    biases = tuple(own[name] for name in ("b_ada", "b_qv", "b_proj", "b_fc1", "b_fc2"))
    result = run_step(args + (packed, own["fc2"]) + biases, perm)
    act, glat, *rest = finish(*result, [w.shape for w in weights])
    return (act.reshape(SLOTS, LEN, D), glat.reshape(SLOTS, LEN, D), *rest)


def solution(mesh):
    split0 = (P("dp", None, None), P("dp", None), P("dp", None, None), P("dp", None), P("dp"))
    params = (P(None, "dp", None), P(None, "dp")) * 5
    outs = (P("dp", None, None), P("dp", None, None), P("dp", None)) + params
    return jax.shard_map(body, mesh=mesh, in_specs=split0 + params, out_specs=outs, check_vma=False)
```
